256 devices in a mesh: rows: 128 (over x, y_hi, z, core), heads: 2 (over y_lo).
Axes of the slice: x: 4, y: 4 (y_hi: 2, y_lo: 2; y = y_hi * 2 + y_lo), z: 8, core: 2. Of those that a mesh axis runs over, the one named last changes fastest.
Arguments:
- queries: bfloat16 [32768, 2048], P('rows', 'heads'), may hold values from -48 to 48
- keys: bfloat16 [32768, 2048], P('rows', 'heads'), may hold values from -24 to 24
- values: bfloat16 [32768, 2048], P('rows', 'heads'), may hold values from -6 to 6
- summary_cols: int32 [16], replicated, may hold values from 8 to 255, as said below
- w_out: bfloat16 [2048, 2048], P('heads'), may hold values from -1 to 1
Outputs:
- mixed: bfloat16 [32768, 2048], P('rows', 'heads')
The draws below stay inside these ranges and needn't reach their ends.
Inputs may be any that keep to these rules, and one draw needn't show every extreme that they name: `summary_cols`: Rising; entry j lies in columns 16 * j + 8 to 16 * j + 15.
All inputs are finite; a program needn't handle non-finite values.
Results may differ from the reference program's by a relative error of at most 0.014.
Values may be sent and summed in bfloat16 or wider, within the bound.
A program may use at most 64 MiB of HBM per device.

```python
import math
import jax
import jax.numpy as jnp
from jax import lax

D = 2048
HEADS = 16
HEAD_DIM = 128
GRID_COLS = 256
GRID_ROWS = 128
TOKENS = 32768
SUMMARY = 16


def shared_normal(key):
    return jnp.clip(jax.random.normal(key, (TOKENS, D), jnp.float32), -6.0, 6.0)


def column_field(key):
    column_key = jax.random.fold_in(key, 11)
    along = jnp.clip(jax.random.normal(column_key, (GRID_COLS, D), jnp.float32), -6.0, 6.0)
    along = along * math.sqrt(3.0 / math.sqrt(HEAD_DIM))
    return jnp.tile(along, (GRID_ROWS, 1))


def draw_queries(key, part):
    common = column_field(key)
    key = jax.random.fold_in(key, 3)
    drawn = 1.5 * jnp.clip(jax.random.normal(key, (TOKENS, D), jnp.float32), -6.0, 6.0)
    return (drawn + common).astype(jnp.bfloat16)


def draw_keys(key, part):
    base_field = shared_normal(key)
    common = column_field(key)
    field = base_field
    return (field + common).astype(jnp.bfloat16)


def draw_summary_cols(key, part):
    key = jax.random.fold_in(key, 7)
    offsets = jax.random.randint(key, (SUMMARY,), 8, 16, dtype=jnp.int32)
    return jnp.arange(SUMMARY, dtype=jnp.int32) * 16 + offsets


def block_scale(rng, shape, cuts, low, top_value):
    def one(dim, parts):
        heights = jax.random.uniform(jax.random.fold_in(jax.random.fold_in(rng, 6), dim), (parts,), jnp.float32, low / len(cuts), top_value / len(cuts))
        return jnp.repeat(jnp.exp(heights), shape[dim] // parts).reshape((-1,) + (1,) * (len(shape) - dim - 1))

    level = one(*cuts[0])
    for cut in cuts[1:]:
        level = level * one(*cut)
    return level


def gaussian(key, extent, scale, limit, cuts=(), kind=jnp.bfloat16):
    values = scale * jax.random.normal(key, extent, jnp.float32)
    if cuts:
        values = values * block_scale(key, extent, cuts, -0.22, 0.18)
    return jnp.clip(values, -limit, limit).astype(kind)


def setup_inputs(seed: int = 0) -> dict:
    key_list = jax.random.split(jax.random.key(seed), 6)
    return {
        "queries": draw_queries(jax.random.fold_in(key_list[5], 71), 0),
        "keys": draw_keys(jax.random.fold_in(key_list[5], 71), 0),
        "values": gaussian(key_list[2], (TOKENS, D), 1.0, 6.0, ((0, 128), (1, 2))),
        "summary_cols": draw_summary_cols(jax.random.fold_in(key_list[5], 71), 0),
        "w_out": gaussian(key_list[4], (D, D), (D // 64) ** -0.5, 1.0, ((0, 2),)),
    }


negative = -1e+30

def reference(queries, keys, values, summary_cols, w_out):
    inv_root = 1.0 / math.sqrt(HEAD_DIM)
    grid_q = queries.reshape(GRID_ROWS, GRID_COLS, HEADS, HEAD_DIM)
    grid_k = keys.reshape(GRID_ROWS, GRID_COLS, HEADS, HEAD_DIM)
    grid_v = values.reshape(GRID_ROWS, GRID_COLS, HEADS, HEAD_DIM)
    row_index = jnp.arange(GRID_ROWS, dtype=jnp.int32)
    col_index = jnp.arange(GRID_COLS, dtype=jnp.int32)
    col_allowed = row_index[None, :] <= row_index[:, None]

    def column_one(arrays):
        col_q, col_k, col_v = arrays
        scores = jnp.einsum('rhe,she->hrs', col_q.astype(jnp.float32), col_k.astype(jnp.float32)) * inv_root
        scores = jnp.where(col_allowed[None], scores, negative)
        peaks = lax.optimization_barrier(jnp.max(scores, axis=2))
        weights = jnp.where(col_allowed[None], jnp.exp(scores - peaks[..., None]), 0.0)
        totals = lax.optimization_barrier(jnp.sum(weights, axis=2))
        probs = lax.optimization_barrier(weights.astype(jnp.bfloat16))
        summed = jnp.einsum('hrs,she->rhe', probs.astype(jnp.float32), col_v.astype(jnp.float32))
        col_out = (summed / totals.T[..., None]).astype(jnp.bfloat16)
        return (col_out, (peaks + jnp.log(totals)).T)
    col_out, col_lse = lax.map(column_one, (grid_q.transpose(1, 0, 2, 3), grid_k.transpose(1, 0, 2, 3), grid_v.transpose(1, 0, 2, 3)))
    col_out = col_out.transpose(1, 0, 2, 3)
    col_lse = col_lse.transpose(1, 0, 2)
    sum_count = summary_cols.shape[0]
    sum_k = jnp.take(grid_k, summary_cols, axis=1).reshape(GRID_ROWS * sum_count, HEADS, HEAD_DIM).astype(jnp.float32)
    sum_v = jnp.take(grid_v, summary_cols, axis=1).reshape(GRID_ROWS * sum_count, HEADS, HEAD_DIM).astype(jnp.float32)
    key_rows = jnp.repeat(row_index, sum_count)
    key_cols = jnp.tile(summary_cols, GRID_ROWS)
    row_allowed = col_index[None, :] < col_index[:, None]

    def row_one(arrays):
        grid_row, row_q, row_k, row_v, row_col_out, row_col_lse = arrays
        query_f = row_q.astype(jnp.float32)
        near_scores = jnp.einsum('che,khe->hck', query_f, row_k.astype(jnp.float32)) * inv_root
        near_scores = jnp.where(row_allowed[None], near_scores, negative)
        sum_allowed = (key_rows[None, :] < grid_row) & (key_cols[None, :] != col_index[:, None])
        far_scores = jnp.einsum('che,khe->hck', query_f, sum_k) * inv_root
        far_scores = jnp.where(sum_allowed[None], far_scores, negative)
        lse_t = row_col_lse.T
        peaks = jnp.maximum(jnp.maximum(lax.optimization_barrier(jnp.max(near_scores, axis=2)), lax.optimization_barrier(jnp.max(far_scores, axis=2))), lse_t)
        near_w = jnp.where(row_allowed[None], jnp.exp(near_scores - peaks[..., None]), 0.0)
        far_w = jnp.where(sum_allowed[None], jnp.exp(far_scores - peaks[..., None]), 0.0)
        col_w = jnp.exp(lse_t - peaks)
        totals = lax.optimization_barrier(jnp.sum(near_w, axis=2)) + lax.optimization_barrier(jnp.sum(far_w, axis=2)) + col_w
        near_p = lax.optimization_barrier(near_w.astype(jnp.bfloat16)).astype(jnp.float32)
        far_p = lax.optimization_barrier(far_w.astype(jnp.bfloat16)).astype(jnp.float32)
        summed = jnp.einsum('hck,khe->che', near_p, row_v.astype(jnp.float32))
        summed = summed + jnp.einsum('hck,khe->che', far_p, sum_v)
        summed = summed + col_w.T[..., None] * row_col_out.astype(jnp.float32)
        return (summed / totals.T[..., None]).astype(jnp.bfloat16)
    attn = lax.map(row_one, (row_index, grid_q, grid_k, grid_v, col_out, col_lse))
    attn = attn.reshape(TOKENS, D)
    return jnp.dot(attn, w_out, preferred_element_type=jnp.float32).astype(jnp.bfloat16)
```

```python
import math

import jax
import jax.numpy as jnp
from jax import lax
from jax.experimental import pallas as pl
from jax.experimental.pallas import tpu as pltpu
from jax.sharding import PartitionSpec as P

HEAD_DIM = 128
COLS = 256
HALF = 128
SUMS = 16
NZ = 8
NG = 8
MESH = pl.DeviceIdType.MESH
BF, F32 = jnp.bfloat16, jnp.float32
BIG = 1e30
TO_LOG2 = math.log2(math.e) / math.sqrt(HEAD_DIM)


def nt(a, b):
    return lax.dot_general(a, b, (((1,), (1,)), ((), ())), preferred_element_type=F32)


def nn(a, b):
    return jnp.dot(a, b, preferred_element_type=F32)


def iota(shape, dim):
    return lax.broadcasted_iota(jnp.int32, shape, dim)


def body(cols_ref, q_hbm, k_hbm, v_hbm, w_hbm, o_ref, zbuf, pbuf, ybuf, obuf, rbuf, cbuf, abuf, home, wbuf,
         kvl, ssel, sz, sg, qb, ekey, perm, lsrc, lbuf, acc, mx, tot, own, xsend, xrecv,
         zss, zrs, gss, grs, pss, prs, rss, rrs, lss, lrs, ass, ars, xss, xrs, loc):
    me = lax.axis_index("rows")
    t = lax.axis_index("heads")
    c = me % 2
    z = (me // 2) % NZ
    g = me // (2 * NZ)
    p = g * 2 + c

    def row_id(gg, zz, cc):
        return (gg * NZ + zz) * 2 + cc

    def z_mate(s):
        zz = (z + s) % NZ
        return zz, {"rows": row_id(g, zz, c)}

    def remote(src, dst, ssem, rsem, device):
        return pltpu.make_async_remote_copy(
            src_ref=src, dst_ref=dst, send_sem=ssem, recv_sem=rsem, device_id=device, device_id_type=MESH
        )

    def drain(ref, sem):
        pltpu.make_async_copy(ref, ref, sem).wait()

    hbm = (q_hbm, k_hbm, v_hbm)
    kv_loads = [pltpu.make_async_copy(hbm[1 + a], kvl.at[a], loc.at[a]) for a in range(2)]
    for load in kv_loads:
        load.start()
    w_load = pltpu.make_async_copy(w_hbm, wbuf, loc.at[2])

    barrier = pltpu.get_barrier_semaphore()

    @pl.loop(1, NZ)
    def _(s):
        pl.semaphore_signal(barrier, inc=1, device_id=z_mate(s)[1], device_id_type=MESH)

    @pl.loop(1, 2 * NG)
    def _(s):
        d = (p + s) % (2 * NG)
        pl.semaphore_signal(barrier, inc=1, device_id={"rows": row_id(d // 2, z, d % 2)}, device_id_type=MESH)

    pl.semaphore_signal(barrier, inc=1, device_id={"heads": 1 - t}, device_id_type=MESH)

    lane1 = iota((1, HEAD_DIM), 1)
    sub16 = iota((SUMS, COLS), 0)
    as_row = jnp.full((1, HEAD_DIM), -1, jnp.int32)
    as_col = jnp.full((SUMS, COLS), -1, jnp.int32)
    for j in range(SUMS):
        as_row = jnp.where(lane1 == j, cols_ref[j], as_row)
        as_col = jnp.where(sub16 == j, cols_ref[j], as_col)
    pick = jnp.where(iota((SUMS, COLS), 1) == as_col, 1.0, 0.0).astype(BF)

    for load in kv_loads:
        load.wait()
    for a in range(2):
        ssel[a] = nn(pick, kvl[a]).astype(BF)
    pl.semaphore_wait(barrier, NZ - 1 + 2 * NG - 1 + 1)

    def head_lanes(zz):
        return pl.ds(pl.multiple_of(zz * HEAD_DIM, HEAD_DIM), HEAD_DIM)

    pltpu.make_async_copy(ssel.at[:, :, head_lanes(z)], sz.at[:, z], zrs.at[6]).start()

    @pl.loop(1, NZ)
    def _(s):
        zz, device = z_mate(s)
        remote(ssel.at[:, :, head_lanes(zz)], sz.at[:, z], zss.at[6], zrs.at[6], device).start()

    for h in range(2):
        for a in range(3):
            ch = h * 3 + a
            rows = pl.ds(h * HALF, HALF)
            pltpu.make_async_copy(hbm[a].at[rows, head_lanes(z)], zbuf.at[a, z, rows], zrs.at[ch]).start()

            @pl.loop(1, NZ)
            def _(s):
                zz, device = z_mate(s)
                remote(hbm[a].at[rows, head_lanes(zz)], zbuf.at[a, z, rows], zss.at[ch], zrs.at[ch], device).start()

    w_load.start()

    lane = iota((COLS, HEAD_DIM), 1)
    not_own = jnp.where(iota((COLS, HEAD_DIM), 0) == as_row, -BIG, 0.0)
    for zz in range(NZ):
        pos = lane - SUMS
        kz, cc = pos % NZ, pos // NZ
        later = (kz > zz) | ((kz == zz) & (cc >= c))
        in_lanes = (pos >= 0) & (pos < 2 * NZ)
        qb[zz] = jnp.where(in_lanes & later, -BIG, not_own).astype(BF)
    key = iota((COLS, HEAD_DIM), 0)
    for_j = lane == key % SUMS
    for_row = lane == SUMS + key // SUMS
    ekey[0] = jnp.where(for_j, 1.0, 0.0).astype(BF)
    ekey[1] = jnp.where(for_j | for_row, 1.0, 0.0).astype(BF)
    out_i, in_i = iota((COLS, COLS), 0), iota((COLS, COLS), 1)
    perm[...] = jnp.where((out_i // 16 == in_i % 16) & (out_i % 16 == in_i // 16), 1.0, 0.0).astype(BF)
    eye = jnp.where(iota((HALF, HALF), 0) == iota((HALF, HALF), 1), 1.0, 0.0).astype(BF)
    ones = jnp.ones((16, COLS), BF)
    acc[...] = jnp.zeros_like(acc)
    mx[...] = jnp.full_like(mx, -BIG)
    tot[...] = jnp.zeros_like(tot)

    drain(sz, zrs.at[6])
    pltpu.make_async_copy(sz, sg.at[:, p], grs).start()

    @pl.loop(1, 2 * NG)
    def _(s):
        d = (p + s) % (2 * NG)
        remote(sz, sg.at[:, p], gss, grs, {"rows": row_id(d // 2, z, d % 2)}).start()

    def forward(a, h):
        chunk = zbuf.at[a, :, pl.ds(h * HALF, HALF)]
        drain(chunk, zrs.at[h * 3 + a])

        def part(gg):
            return zbuf.at[a, :, pl.ds(pl.multiple_of(h * HALF + gg * 16, 16), 16)]

        @pl.loop(1, NG)
        def _(s):
            gg = (g + s) % NG
            remote(part(gg), pbuf.at[a, p], pss.at[a, h], prs.at[a], {"rows": row_id(gg, z, h)}).start()

        @pl.when(c == h)
        def _():
            pltpu.make_async_copy(part(g), pbuf.at[a, p], prs.at[a]).start()

        @pl.when(c != h)
        def _():
            remote(part(g), pbuf.at[a, p], pss.at[a, h], prs.at[a], {"rows": row_id(g, z, h)}).start()

    def update(h, i, lanes, s, vt):
        old = mx[h, i, :1, lanes]
        new = jnp.maximum(old, jnp.max(s, axis=0, keepdims=True))
        shrink = jnp.exp2(old - new)
        got = nn(vt, jnp.exp2(s - new).astype(BF))
        acc[h, i, :, lanes] = acc[h, i, :, lanes] * shrink + got[:HEAD_DIM]
        tot[h, i, :1, lanes] = tot[h, i, :1, lanes] * shrink + got[HEAD_DIM : HEAD_DIM + 1]
        mx[h, i, :1, lanes] = new

    def summary(h):
        @pl.loop(0, g + 1)
        def _(gg):
            keys = sg[0, pl.ds(2 * gg, 2)].reshape(COLS, HEAD_DIM)
            vals = sg[1, pl.ds(2 * gg, 2)].reshape(COLS, HEAD_DIM)
            keys = jnp.concatenate([keys, ekey[(gg == g).astype(jnp.int32)]], axis=1)
            vt = jnp.concatenate([nt(eye, vals).astype(BF), ones], axis=0)
            for i in range(NZ // 2):
                rows = (slice(2 * i, 2 * i + 2), slice(h * HALF, (h + 1) * HALF))
                qs = jnp.concatenate(
                    [zbuf[0, rows[0], rows[1]].reshape(COLS, HEAD_DIM), qb[rows[0], rows[1]].reshape(COLS, HEAD_DIM)],
                    axis=1,
                )
                update(h, i, slice(0, COLS), nt(keys, qs) * TO_LOG2, vt)

    def near(h):
        n = HALF * (h + 1)
        before = iota((n, HALF), 0) < iota((n, HALF), 1) + h * HALF

        @pl.loop(0, NZ // 2)
        def _(i):
            for e in range(2):
                zz = 2 * i + e
                s = nt(zbuf[1, zz, :n], zbuf[0, zz, h * HALF : (h + 1) * HALF]) * TO_LOG2
                s = jnp.where(before, s, -BIG)
                vt = jnp.concatenate([nt(eye, zbuf[2, zz, :n]).astype(BF), ones[:, :n]], axis=0)
                update(h, i, slice(e * HALF, (e + 1) * HALF), s, vt)

    def column(h):
        @pl.when(c == h)
        def _():
            for a in range(3):
                drain(pbuf.at[a], prs.at[a])

                @pl.loop(0, NG)
                def _(gg):
                    y = nn(perm[...], pbuf[a, pl.ds(2 * gg, 2)].reshape(COLS, HEAD_DIM))
                    ybuf[a, :, gg] = y.astype(BF).reshape(16, 16, HEAD_DIM)

            def row_of(i):
                return (i // 16) * 16 + (i % 8) * 2 + (i // 8) % 2

            sh = (HALF, HALF)
            causal = row_of(iota(sh, 1)) <= row_of(iota(sh, 0))
            own_lane = iota(sh, 1) - g * 16
            one = jnp.ones(sh, BF)

            @pl.loop(0, 16)
            def _(i):
                qc, kc, vc = (ybuf[a, i].reshape(HALF, HEAD_DIM) for a in range(3))
                s = jnp.where(causal, nt(qc, kc) * TO_LOG2, -BIG)
                peak = jnp.max(s, axis=1, keepdims=True)
                w = jnp.exp2(s - peak).astype(BF)
                got = nn(w, jnp.concatenate([vc, one], axis=1))
                total = got[:, HEAD_DIM:]
                obuf[i] = (got[:, :HEAD_DIM] / total).astype(BF).reshape(NG, 16, HEAD_DIM)
                lse = peak + jnp.log2(total)
                lsrc[...] = jnp.where(own_lane == i, lse, jnp.where(i == 0, 0.0, lsrc[...]))

            def give_back(gg):
                x = nn(perm[...], obuf[:, gg].reshape(COLS, HEAD_DIM))
                rbuf[pl.ds(2 * gg, 2)] = x.astype(BF).reshape(2, NZ, 16, HEAD_DIM)

            def send_back(gg, cc):
                d = gg * 2 + cc
                device = {"rows": row_id(gg, z, cc)}
                tile = lsrc.at[pl.ds(pl.multiple_of(d * NZ, NZ), NZ)]
                remote(rbuf.at[d], cbuf.at[h, g], rss, rrs.at[h], device).start()
                remote(tile, lbuf.at[h, g], lss, lrs.at[h], device).start()

            @pl.loop(1, NG)
            def _(s):
                gg = (g + s) % NG
                give_back(gg)
                for cc in range(2):
                    send_back(gg, cc)

            give_back(g)
            send_back(g, 1 - h)
            pltpu.make_async_copy(rbuf.at[p], cbuf.at[h, g], rrs.at[h]).start()
            tile = lsrc.at[pl.ds(pl.multiple_of(p * NZ, NZ), NZ)]
            pltpu.make_async_copy(tile, lbuf.at[h, g], lrs.at[h]).start()

    def merge(h):
        drain(cbuf.at[h], rrs.at[h])
        drain(lbuf.at[h], lrs.at[h])
        lse_all = jnp.sum(lbuf[h], axis=0)
        rows = slice(h * HALF, (h + 1) * HALF)
        for zz in range(NZ):
            lanes = slice((zz % 2) * HALF, (zz % 2 + 1) * HALF)
            lse = lse_all[zz : zz + 1]
            m = mx[h, zz // 2, :1, lanes]
            peak = jnp.maximum(m, lse)
            near_w = jnp.exp2(m - peak)
            col_w = jnp.exp2(lse - peak)
            inv = 1.0 / (tot[h, zz // 2, :1, lanes] * near_w + col_w)
            col_t = nt(eye, cbuf[h, :, zz].reshape(HALF, HEAD_DIM))
            out_t = acc[h, zz // 2, :, lanes] * (near_w * inv) + col_t * (col_w * inv)
            abuf[zz, rows] = nt(eye, out_t.astype(BF)).astype(BF)
        rows = pl.ds(h * HALF, HALF)
        pltpu.make_async_copy(abuf.at[z, rows], home.at[rows, head_lanes(z)], ars.at[h]).start()

        @pl.loop(1, NZ)
        def _(s):
            zz, device = z_mate(s)
            remote(abuf.at[zz, rows], home.at[rows, head_lanes(z)], ass.at[h], ars.at[h], device).start()

    width = NZ * HEAD_DIM

    def project(h):
        rows = pl.ds(h * HALF, HALF)
        drain(home.at[rows], ars.at[h])
        theirs = pl.ds(pl.multiple_of((1 - t) * width, width), width)
        ours = pl.ds(pl.multiple_of(t * width, width), width)
        xsend[h] = nn(home[rows], wbuf[:, theirs]).astype(BF)
        remote(xsend.at[h], xrecv.at[h], xss.at[h], xrs.at[h], {"heads": 1 - t}).start()
        own[h] = nn(home[rows], wbuf[:, ours])

    def finish(h):
        drain(xrecv.at[h], xrs.at[h])
        o_ref[pl.ds(h * HALF, HALF)] = (own[h] + xrecv[h].astype(F32)).astype(BF)

    for a in range(3):
        forward(a, 0)
    drain(sg, grs)
    near(0)
    column(0)
    forward(0, 1)
    summary(0)
    forward(1, 1)
    merge(0)
    summary(1)
    forward(2, 1)
    near(1)
    column(1)
    w_load.wait()
    project(0)
    merge(1)
    project(1)
    finish(0)
    finish(1)

    drain(sz.at[:, pl.ds(0, NZ - 1)], zss.at[6])
    drain(sg.at[:, pl.ds(0, 2 * NG - 1)], gss)
    for h in range(2):
        rows = pl.ds(h * HALF, HALF)
        for a in range(3):
            drain(zbuf.at[a, pl.ds(0, NZ - 1), rows], zss.at[h * 3 + a])

            @pl.when(c == h)
            def _():
                drain(pbuf.at[a, pl.ds(0, NG - 1)], pss.at[a, h])

            @pl.when(c != h)
            def _():
                drain(pbuf.at[a, pl.ds(0, NG)], pss.at[a, h])

        drain(abuf.at[pl.ds(0, NZ - 1), rows], ass.at[h])
        drain(xsend.at[h], xss.at[h])
    drain(rbuf.at[pl.ds(0, 2 * NG - 1)], rss)
    drain(lsrc.at[pl.ds(0, (2 * NG - 1) * NZ)], lss)


def on_device(queries, keys, values, summary_cols, w_out):
    width = queries.shape[1]
    any_space = pl.BlockSpec(memory_space=pl.ANY)
    dma = pltpu.SemaphoreType.DMA
    vmem = pltpu.VMEM
    e = HEAD_DIM
    return pl.pallas_call(
        body,
        out_shape=jax.ShapeDtypeStruct(queries.shape, BF),
        in_specs=[pl.BlockSpec(memory_space=pltpu.SMEM)] + [any_space] * 4,
        out_specs=pl.BlockSpec(memory_space=pltpu.VMEM),
        scratch_shapes=[
            vmem((3, NZ, COLS, e), BF),
            vmem((3, 2 * NG, NZ, 16, e), BF),
            vmem((3, 16, NG, 16, e), BF),
            vmem((16, NG, 16, e), BF),
            vmem((2 * NG, NZ, 16, e), BF),
            vmem((2, NG, NZ, 16, e), BF),
            vmem((NZ, COLS, e), BF),
            vmem((COLS, width), BF),
            vmem(w_out.shape, BF),
            vmem((2, COLS, width), BF),
            vmem((2, SUMS, width), BF),
            vmem((2, NZ, SUMS, e), BF),
            vmem((2, 2 * NG, NZ, SUMS, e), BF),
            vmem((NZ, COLS, e), BF),
            vmem((2, COLS, e), BF),
            vmem((COLS, COLS), BF),
            vmem((HALF, e), F32),
            vmem((2, NG, NZ, e), F32),
            vmem((2, NZ // 2, e, COLS), F32),
            vmem((2, NZ // 2, 8, COLS), F32),
            vmem((2, NZ // 2, 8, COLS), F32),
            vmem((2, HALF, width), F32),
            vmem((2, HALF, width), BF),
            vmem((2, HALF, width), BF),
            dma((7,)), dma((7,)),
            dma, dma,
            dma((3, 2)), dma((3,)),
            dma, dma((2,)),
            dma, dma((2,)),
            dma((2,)), dma((2,)),
            dma((2,)), dma((2,)),
            dma((3,)),
        ],
        name="strided_attention",
        compiler_params=pltpu.CompilerParams(
            collective_id=0, has_side_effects=True, vmem_limit_bytes=48 * 1024 * 1024
        ),
    )(summary_cols, queries, keys, values, w_out)


def solution(mesh):
    return jax.shard_map(
        on_device,
        mesh=mesh,
        in_specs=(P("rows", "heads"), P("rows", "heads"), P("rows", "heads"), P(), P("heads", None)),
        out_specs=P("rows", "heads"),
        check_vma=False,
    )
```

```python
import math

import jax
import jax.numpy as jnp
from jax import lax
from jax.experimental import pallas as pl
from jax.experimental.pallas import tpu as pltpu
from jax.sharding import PartitionSpec as P

HEAD_DIM = 128
COLS = 256
SUMS = 16
NZ = 8
NG = 8
BLOCK = 16
LANES = 256
STAGES = ((0, 8, 128), (8, 4, 64), (12, 4, 64))
UNROLL = 16
NEXT = ((3, 4), (5, 6), (7, 8))
MESH = pl.DeviceIdType.MESH
BF, F32 = jnp.bfloat16, jnp.float32
BIG = 1e30
TO_LOG2 = math.log2(math.e) / math.sqrt(HEAD_DIM)


def nt(a, b):
    return lax.dot_general(a, b, (((1,), (1,)), ((), ())), preferred_element_type=F32)


def nn(a, b):
    return jnp.dot(a, b, preferred_element_type=F32)


def iota(shape, dim):
    return lax.broadcasted_iota(jnp.int32, shape, dim)


def body(cols_ref, q_hbm, k_hbm, v_hbm, w_hbm, o_ref, zbuf, pbuf, ybuf, wts, obuf, rbuf, cbuf, abuf, home, wbuf,
         kvl, ssel, sz, sg, qb, ekey, perm, lsrc, lbuf, acc, mx, tot, own, xsend, xrecv,
         zss, zrs, gss, grs, pss, prs, rss, rrs, lss, lrs, ass, ars, xss, xrs, loc):
    me = lax.axis_index("rows")
    t = lax.axis_index("heads")
    c = lax.rem(me, 2)
    z = lax.rem(lax.div(me, 2), NZ)
    g = lax.div(me, 2 * NZ)
    p = g * 2 + c
    x, y_hi = lax.div(g, 2), lax.rem(g, 2)
    odd_x = lax.rem(x, 2)

    def row_id(gg, zz, cc):
        return (gg * NZ + zz) * 2 + cc

    def z_mate(s):
        zz = lax.rem(z + s, NZ)
        return zz, {"rows": row_id(g, zz, c)}

    def each_z_mate(act):
        @pl.loop(1, NZ // 2)
        def _(s):
            act(*z_mate(s))
            act(*z_mate(NZ - s))

        act(*z_mate(NZ // 2))

    def remote(src, dst, ssem, rsem, device):
        return pltpu.make_async_remote_copy(
            src_ref=src, dst_ref=dst, send_sem=ssem, recv_sem=rsem, device_id=device, device_id_type=MESH
        )

    def local(src, dst, sem):
        pltpu.make_async_copy(src, dst, sem).start()

    def drain(ref, sem):
        pltpu.make_async_copy(ref, ref, sem).wait()

    def owner(st, k):
        if st == 0:
            return k, 0
        return 2 * k + (lax.rem(k, 2) if st == 1 else 1 - lax.rem(k, 2)), 1

    def mine(st):
        if st == 0:
            return c == 0
        return (c == 1) & (y_hi == (odd_x if st == 1 else 1 - odd_x))

    def my_block(st):
        return g if st == 0 else x

    def stage_cols(st):
        return pl.ds(STAGES[st][0] * BLOCK, STAGES[st][2])

    hbm = (q_hbm, k_hbm, v_hbm)
    kv_loads = [pltpu.make_async_copy(hbm[1 + a], kvl.at[a], loc.at[a]) for a in range(2)]
    barrier = pltpu.get_barrier_semaphore()

    @pl.loop(1, NZ)
    def _(s):
        pl.semaphore_signal(barrier, inc=1, device_id=z_mate(s)[1], device_id_type=MESH)

    @pl.loop(1, 2 * NG)
    def _(s):
        d = lax.rem(p + s, 2 * NG)
        device = {"rows": row_id(lax.div(d, 2), z, lax.rem(d, 2))}
        pl.semaphore_signal(barrier, inc=1, device_id=device, device_id_type=MESH)

    pl.semaphore_signal(barrier, inc=1, device_id={"heads": 1 - t}, device_id_type=MESH)
    for load in kv_loads:
        load.start()
    w_load = pltpu.make_async_copy(w_hbm, wbuf, loc.at[2])

    def head_lanes(zz):
        return pl.ds(pl.multiple_of(zz * HEAD_DIM, HEAD_DIM), HEAD_DIM)

    chunks = 3 * len(STAGES)

    def start_chunk(ch):
        st, a = ch // 3, ch % 3
        rows = stage_cols(st)
        local(hbm[a].at[rows, head_lanes(z)], zbuf.at[a, z, rows], zrs.at[ch])

        @each_z_mate
        def _(zz, device):
            remote(hbm[a].at[rows, head_lanes(zz)], zbuf.at[a, z, rows], zss.at[ch], zrs.at[ch], device).start()

    def chunk_left(ch):
        drain(zbuf.at[ch % 3, pl.ds(0, NZ - 1), stage_cols(ch // 3)], zss.at[ch])

    pl.semaphore_wait(barrier, NZ - 1 + 2 * NG - 1 + 1)

    start_chunk(0)

    lane1 = iota((1, HEAD_DIM), 1)
    sub16 = iota((SUMS, COLS), 0)
    as_row = jnp.full((1, HEAD_DIM), -1, jnp.int32)
    as_col = jnp.full((SUMS, COLS), -1, jnp.int32)
    for j in range(SUMS):
        as_row = jnp.where(lane1 == j, cols_ref[j], as_row)
        as_col = jnp.where(sub16 == j, cols_ref[j], as_col)
    pick = jnp.where(iota((SUMS, COLS), 1) == as_col, 1.0, 0.0).astype(BF)
    for a, load in enumerate(kv_loads):
        load.wait()
        ssel[a] = nn(pick, kvl[a]).astype(BF)

    local(ssel.at[:, :, head_lanes(z)], sz.at[:, z], zrs.at[chunks])

    @each_z_mate
    def _(zz, device):
        remote(ssel.at[:, :, head_lanes(zz)], sz.at[:, z], zss.at[chunks], zrs.at[chunks], device).start()

    for ch in range(1, len(NEXT)):
        start_chunk(ch)
    w_load.start()

    lane = iota((COLS, HEAD_DIM), 1)
    not_own = jnp.where(iota((COLS, HEAD_DIM), 0) == as_row, -BIG, 0.0)
    for zz in range(NZ):
        pos = lane - SUMS
        kz, cc = pos % NZ, pos // NZ
        later = (kz > zz) | ((kz == zz) & (cc >= c))
        in_lanes = (pos >= 0) & (pos < 2 * NZ)
        qb[zz] = jnp.where(in_lanes & later, -BIG, not_own).astype(BF)
    key = iota((COLS, HEAD_DIM), 0)
    for_j = lane == key % SUMS
    for_row = lane == SUMS + key // SUMS
    ekey[0] = jnp.where(for_j, 1.0, 0.0).astype(BF)
    ekey[1] = jnp.where(for_j | for_row, 1.0, 0.0).astype(BF)
    out_i, in_i = iota((COLS, COLS), 0), iota((COLS, COLS), 1)
    perm[...] = jnp.where((out_i // 16 == in_i % 16) & (out_i % 16 == in_i // 16), 1.0, 0.0).astype(BF)
    eye = jnp.where(out_i == in_i, 1.0, 0.0).astype(BF)
    eye1 = eye[:HEAD_DIM, :HEAD_DIM]
    ones = jnp.ones((16, 2 * COLS), BF)
    acc[...] = jnp.zeros_like(acc)
    mx[...] = jnp.full_like(mx, -BIG)
    tot[...] = jnp.zeros_like(tot)

    def share_summary():
        drain(sz, zrs.at[chunks])
        local(sz, sg.at[c, :, g], grs.at[0])

        @pl.loop(1, NG)
        def _(s):
            remote(sz, sg.at[c, :, g], gss.at[0], grs.at[0], {"rows": row_id(lax.rem(g + s, NG), z, c)}).start()

    def share_summary_cores():
        drain(sg.at[c], grs.at[0])
        remote(sg.at[c], sg.at[c], gss.at[1], grs.at[1], {"rows": row_id(g, z, 1 - c)}).start()

    def forward(a, st):
        ch = st * 3 + a
        drain(zbuf.at[a, :, stage_cols(st)], zrs.at[ch])
        if ch < len(NEXT):
            chunk_left(ch)
            for later in NEXT[ch]:
                start_chunk(later)
        first, count, _w = STAGES[st]

        def part(k):
            return zbuf.at[a, :, pl.ds(pl.multiple_of((first + k) * BLOCK, BLOCK), BLOCK)]

        def send(k):
            gg, cc = owner(st, k)
            remote(part(k), pbuf.at[a, p], pss.at[a, st], prs.at[a], {"rows": row_id(gg, z, cc)}).start()

        k0 = my_block(st)

        @pl.loop(1, count)
        def _(s):
            send(lax.rem(k0 + s, count))

        @pl.when(mine(st))
        def _():
            local(part(k0), pbuf.at[a, p], prs.at[a])

        @pl.when(jnp.logical_not(mine(st)))
        def _():
            send(k0)

    def update(st, i, lanes, s, vt):
        old = mx[st, i, :1, lanes]
        new = jnp.maximum(old, jnp.max(s, axis=0, keepdims=True))
        shrink = jnp.exp2(old - new)
        got = nn(vt, jnp.exp2(s - new).astype(BF))
        acc[st, i, :, lanes] = acc[st, i, :, lanes] * shrink + got[:HEAD_DIM]
        tot[st, i, :1, lanes] = tot[st, i, :1, lanes] * shrink + got[HEAD_DIM : HEAD_DIM + 1]
        mx[st, i, :1, lanes] = new

    def static_cols(st):
        return slice(STAGES[st][0] * BLOCK, STAGES[st][0] * BLOCK + STAGES[st][2])

    def summary(st, part=0, parts=1):
        per = LANES // STAGES[st][2]

        @pl.loop(lax.div((g + 1) * part, parts), lax.div((g + 1) * (part + 1), parts))
        def _(gg):
            keys = jnp.concatenate([sg[cc, 0, gg].reshape(HEAD_DIM, HEAD_DIM) for cc in range(2)], axis=0)
            vals = jnp.concatenate([sg[cc, 1, gg].reshape(HEAD_DIM, HEAD_DIM) for cc in range(2)], axis=0)
            keys = jnp.concatenate([keys, ekey[(gg == g).astype(jnp.int32)]], axis=1)
            vt = jnp.concatenate([nt(eye1, vals).astype(BF), ones[:, :COLS]], axis=0)
            for i in range(NZ // per):
                rows = slice(per * i, per * i + per)
                qs = [r.reshape(LANES, HEAD_DIM) for r in (zbuf[0, rows, static_cols(st)], qb[rows, static_cols(st)])]
                update(st, i, slice(0, LANES), nt(keys, jnp.concatenate(qs, axis=1)) * TO_LOG2, vt)

    def near(st):
        width = STAGES[st][2]
        n = STAGES[st][0] * BLOCK + width
        per = HEAD_DIM // width
        ki, qi = iota((per * n, HEAD_DIM), 0), iota((per * n, HEAD_DIM), 1)
        before = ki % n if per == 1 else jnp.where(ki >= n, ki - n, ki)
        before = before < qi % width + STAGES[st][0] * BLOCK
        if per > 1:
            before = before & ((ki >= n) == (qi >= width))

        @pl.loop(0, NZ // per // 2)
        def _(i):
            for e in range(2):
                rows = pl.ds((2 * i + e) * per, per)
                s = nt(
                    zbuf[1, rows, :n].reshape(per * n, HEAD_DIM),
                    zbuf[0, rows, static_cols(st)].reshape(HEAD_DIM, HEAD_DIM),
                )
                s = jnp.where(before, s * TO_LOG2, -BIG)
                vt = nt(eye1, zbuf[2, rows, :n].reshape(per * n, HEAD_DIM)).astype(BF)
                vt = jnp.concatenate([vt, ones[:, : per * n]], axis=0)
                update(st, i, slice(e * HEAD_DIM, (e + 1) * HEAD_DIM), s, vt)

    sh = (HEAD_DIM, HEAD_DIM)

    def by_column(a):
        drain(pbuf.at[a], prs.at[a])

        @pl.loop(0, NG, unroll=NG)
        def _(gg):
            y = nn(perm[...], pbuf[a, pl.ds(2 * gg, 2)].reshape(COLS, HEAD_DIM))
            ybuf[a, :, gg] = y.astype(BF).reshape(BLOCK, 16, HEAD_DIM)

    def lse_lane(st, i):
        at = my_block(st) * BLOCK + i
        if STAGES[st][2] < HEAD_DIM:
            at = at + (iota(sh, 0) % 2) * STAGES[st][2]
        return iota(sh, 1) == at

    def column_weights(st):
        @pl.when(mine(st))
        def _():
            by_column(0)
            by_column(1)

            def row_of(i):
                return (i // 16) * 16 + (i % 8) * 2 + (i // 8) % 2

            causal = row_of(iota(sh, 1)) <= row_of(iota(sh, 0))
            lsrc[...] = jnp.zeros_like(lsrc)

            @pl.loop(0, BLOCK, unroll=UNROLL)
            def _(i):
                qc, kc = (ybuf[a, i].reshape(sh) for a in range(2))
                s = jnp.where(causal, nt(qc, kc) * TO_LOG2, -BIG)
                peak = jnp.max(s, axis=1, keepdims=True)
                wts[i] = jnp.exp2(s - peak).astype(BF)
                lsrc[...] = jnp.where(lse_lane(st, i), peak, lsrc[...])

    def column_values(st):
        first, count, _w = STAGES[st]

        @pl.when(mine(st))
        def _():
            by_column(2)
            one = jnp.ones(sh, BF)

            @pl.loop(0, BLOCK, unroll=UNROLL)
            def _(i):
                got = nn(wts[i], jnp.concatenate([ybuf[2, i].reshape(sh), one], axis=1))
                total = got[:, HEAD_DIM:]
                obuf[i] = (got[:, :HEAD_DIM] / total).astype(BF).reshape(NG, 16, HEAD_DIM)
                lsrc[...] = lsrc[...] + jnp.where(lse_lane(st, i), jnp.log2(total), 0.0)

            b = first + my_block(st)

            def give_back(gg):
                y = nn(perm[...], obuf[:, gg].reshape(COLS, HEAD_DIM))
                rbuf[pl.ds(2 * gg, 2)] = y.astype(BF).reshape(2, NZ, BLOCK, HEAD_DIM)

            def tile(d):
                return lsrc.at[pl.ds(pl.multiple_of(d * NZ, NZ), NZ)]

            def send_back(gg, cc):
                d = gg * 2 + cc
                device = {"rows": row_id(gg, z, cc)}
                remote(tile(d), lbuf.at[b], lss, lrs.at[st], device).start()
                remote(rbuf.at[d], cbuf.at[b], rss, rrs.at[st], device).start()

            @pl.loop(1, NG)
            def _(s):
                gg = lax.rem(g + s, NG)
                give_back(gg)
                for cc in range(2):
                    send_back(gg, cc)

            give_back(g)
            send_back(g, 1 - c)
            local(rbuf.at[p], cbuf.at[b], rrs.at[st])
            local(tile(p), lbuf.at[b], lrs.at[st])

    def merge(st):
        first, count, width = STAGES[st]
        drain(lbuf.at[pl.ds(first, count)], lrs.at[st])
        drain(cbuf.at[pl.ds(first, count)], rrs.at[st])
        lse_all = jnp.sum(lbuf[first : first + count], axis=0)
        per = LANES // width
        for i in range(NZ // per):
            rows = range(per * i, per * i + per)
            lse = [lse_all[zz : zz + 1] for zz in rows]
            if per > 2:
                lse = [lse[0] + lse[1], lse[2] + lse[3]]
            lse = jnp.concatenate(lse, axis=1)
            m = mx[st, i, :1]
            peak = jnp.maximum(m, lse)
            near_w = jnp.exp2(m - peak)
            col_w = jnp.exp2(lse - peak)
            inv = 1.0 / (tot[st, i, :1] * near_w + col_w)
            col = [cbuf[first : first + count, zz].reshape(width, HEAD_DIM) for zz in rows]
            col_t = nt(eye1, jnp.concatenate(col, axis=0))
            out_t = acc[st, i] * (near_w * inv) + col_t * (col_w * inv)
            out = nt(eye, out_t.astype(BF)).astype(BF)
            abuf[per * i : per * i + per, static_cols(st)] = out.reshape(per, width, HEAD_DIM)
        cols = stage_cols(st)
        local(abuf.at[z, cols], home.at[cols, head_lanes(z)], ars.at[st])

        @each_z_mate
        def _(zz, device):
            remote(abuf.at[zz, cols], home.at[cols, head_lanes(z)], ass.at[st], ars.at[st], device).start()

    width = NZ * HEAD_DIM

    def project(st):
        cols = stage_cols(st)
        drain(home.at[cols], ars.at[st])
        theirs = pl.ds(pl.multiple_of((1 - t) * width, width), width)
        ours = pl.ds(pl.multiple_of(t * width, width), width)
        xsend[cols] = nn(home[cols], wbuf[:, theirs]).astype(BF)
        remote(xsend.at[cols], xrecv.at[cols], xss.at[st], xrs.at[st], {"heads": 1 - t}).start()
        own[cols] = nn(home[cols], wbuf[:, ours])

    def finish(st):
        cols = stage_cols(st)
        drain(xrecv.at[cols], xrs.at[st])
        o_ref[cols] = (own[cols] + xrecv[cols].astype(F32)).astype(BF)

    Q, K, V = range(3)
    share_summary()
    forward(Q, 0)
    forward(K, 0)
    share_summary_cores()
    forward(V, 0)
    near(0)
    drain(sg.at[1 - c], grs.at[1])
    column_weights(0)
    forward(Q, 1)
    summary(0, 0, 2)
    forward(K, 1)
    column_values(0)
    forward(V, 1)
    summary(0, 1, 2)
    forward(Q, 2)
    column_weights(1)
    forward(K, 2)
    near(1)
    merge(0)
    column_values(1)
    forward(V, 2)
    column_weights(2)
    summary(1)
    column_values(2)
    merge(1)
    summary(2)
    near(2)
    w_load.wait()
    project(0)
    merge(2)
    project(1)
    finish(0)
    project(2)
    finish(1)
    finish(2)

    drain(sz.at[:, pl.ds(0, NZ - 1)], zss.at[chunks])
    drain(sg.at[0, :, pl.ds(0, NG - 1)], gss.at[0])
    drain(sg.at[c], gss.at[1])
    for ch in range(len(NEXT), chunks):
        chunk_left(ch)
    for st, (first, count, _w) in enumerate(STAGES):
        for a in range(3):

            @pl.when(mine(st))
            def _():
                drain(pbuf.at[a, pl.ds(0, count - 1)], pss.at[a, st])

            @pl.when(jnp.logical_not(mine(st)))
            def _():
                drain(pbuf.at[a, pl.ds(0, count)], pss.at[a, st])

        cols = stage_cols(st)
        drain(abuf.at[pl.ds(0, NZ - 1), cols], ass.at[st])
        drain(xsend.at[cols], xss.at[st])
    drain(rbuf.at[pl.ds(0, 2 * NG - 1)], rss)
    drain(lsrc.at[pl.ds(0, (2 * NG - 1) * NZ)], lss)


def on_device(queries, keys, values, summary_cols, w_out):
    width = queries.shape[1]
    any_space = pl.BlockSpec(memory_space=pl.ANY)
    dma = pltpu.SemaphoreType.DMA
    vmem = pltpu.VMEM
    e = HEAD_DIM
    n = len(STAGES)
    return pl.pallas_call(
        body,
        out_shape=jax.ShapeDtypeStruct(queries.shape, BF),
        in_specs=[pl.BlockSpec(memory_space=pltpu.SMEM)] + [any_space] * 4,
        out_specs=pl.BlockSpec(memory_space=pltpu.VMEM),
        scratch_shapes=[
            vmem((3, NZ, COLS, e), BF),
            vmem((3, 2 * NG, NZ, BLOCK, e), BF),
            vmem((3, BLOCK, NG, 16, e), BF),
            vmem((BLOCK, e, e), BF),
            vmem((BLOCK, NG, 16, e), BF),
            vmem((2 * NG, NZ, BLOCK, e), BF),
            vmem((2 * NG, NZ, BLOCK, e), BF),
            vmem((NZ, COLS, e), BF),
            vmem((COLS, width), BF),
            vmem(w_out.shape, BF),
            vmem((2, COLS, width), BF),
            vmem((2, SUMS, width), BF),
            vmem((2, NZ, SUMS, e), BF),
            vmem((2, 2, NG, NZ, SUMS, e), BF),
            vmem((NZ, COLS, e), BF),
            vmem((2, COLS, e), BF),
            vmem((COLS, COLS), BF),
            vmem((e, e), F32),
            vmem((2 * NG, NZ, e), F32),
            vmem((n, NZ // 2, e, LANES), F32),
            vmem((n, NZ // 2, 8, LANES), F32),
            vmem((n, NZ // 2, 8, LANES), F32),
            vmem((COLS, width), F32),
            vmem((COLS, width), BF),
            vmem((COLS, width), BF),
            dma((3 * n + 1,)), dma((3 * n + 1,)),
            dma((2,)), dma((2,)),
            dma((3, n)), dma((3,)),
            dma, dma((n,)),
            dma, dma((n,)),
            dma((n,)), dma((n,)),
            dma((n,)), dma((n,)),
            dma((3,)),
        ],
        name="strided_attention",
        compiler_params=pltpu.CompilerParams(
            collective_id=0, has_side_effects=True, vmem_limit_bytes=62 * 1024 * 1024
        ),
    )(summary_cols, queries, keys, values, w_out)


def solution(mesh):
    return jax.shard_map(
        on_device,
        mesh=mesh,
        in_specs=(P("rows", "heads"), P("rows", "heads"), P("rows", "heads"), P(), P("heads", None)),
        out_specs=P("rows", "heads"),
        check_vma=False,
    )
```

```python
import math

import jax
import jax.numpy as jnp
from jax import lax
from jax.experimental import pallas as pl
from jax.experimental.pallas import tpu as pltpu
from jax.sharding import PartitionSpec as P

HEAD_DIM = 128
COLS = 256
SUMS = 16
NZ = 8
NG = 8
BLOCK = 16
LANES = 256
STAGES = ((0, 8, 128), (8, 4, 64), (12, 4, 64))
UNROLL = 16
NEXT = ((3,), (4,), (5,), (6,), (7,), (8,))
MESH = pl.DeviceIdType.MESH
BF, F32 = jnp.bfloat16, jnp.float32
BIG = 1e30
TO_LOG2 = math.log2(math.e) / math.sqrt(HEAD_DIM)


def nt(a, b):
    return lax.dot_general(a, b, (((1,), (1,)), ((), ())), preferred_element_type=F32)


def nn(a, b):
    return jnp.dot(a, b, preferred_element_type=F32)


def iota(shape, dim):
    return lax.broadcasted_iota(jnp.int32, shape, dim)


def body(cols_ref, q_hbm, k_hbm, v_hbm, w_hbm, o_ref, zbuf, pbuf, ybuf, wts, obuf, rbuf, cbuf, abuf, home, wbuf,
         kvl, ssel, sz, sg, qb, ekey, perm, lsrc, lbuf, acc, mx, tot, own, xsend, xrecv, res,
         zss, zrs, gss, grs, pss, prs, rss, rrs, lss, lrs, ass, ars, xss, xrs, loc):
    me = lax.axis_index("rows")
    t = lax.axis_index("heads")
    c = lax.rem(me, 2)
    z = lax.rem(lax.div(me, 2), NZ)
    g = lax.div(me, 2 * NZ)
    p = g * 2 + c
    x, y_hi = lax.div(g, 2), lax.rem(g, 2)
    odd_x = lax.rem(x, 2)

    def row_id(gg, zz, cc):
        return (gg * NZ + zz) * 2 + cc

    def z_mate(s):
        zz = lax.rem(z + s, NZ)
        return zz, {"rows": row_id(g, zz, c)}

    def each_z_mate(act):
        @pl.loop(1, NZ // 2)
        def _(s):
            act(*z_mate(s))
            act(*z_mate(NZ - s))

        act(*z_mate(NZ // 2))

    def remote(src, dst, ssem, rsem, device):
        return pltpu.make_async_remote_copy(
            src_ref=src, dst_ref=dst, send_sem=ssem, recv_sem=rsem, device_id=device, device_id_type=MESH
        )

    def local(src, dst, sem):
        pltpu.make_async_copy(src, dst, sem).start()

    def drain(ref, sem):
        pltpu.make_async_copy(ref, ref, sem).wait()

    def owner(st, k):
        if st == 0:
            return k, 0
        return 4 * lax.div(k, 2) + 2 * (st - 1) + lax.rem(k, 2), 1

    def mine(st):
        if st == 0:
            return c == 0
        return (c == 1) & (odd_x == st - 1)

    def my_block(st):
        return g if st == 0 else 2 * lax.div(x, 2) + y_hi

    def stage_cols(st):
        return pl.ds(STAGES[st][0] * BLOCK, STAGES[st][2])

    hbm = (q_hbm, k_hbm, v_hbm)
    kv_loads = [pltpu.make_async_copy(hbm[1 + a], kvl.at[a], loc.at[a]) for a in range(2)]
    barrier = pltpu.get_barrier_semaphore()

    @pl.loop(1, NZ)
    def _(s):
        pl.semaphore_signal(barrier, inc=1, device_id=z_mate(s)[1], device_id_type=MESH)

    @pl.loop(1, 2 * NG)
    def _(s):
        d = lax.rem(p + s, 2 * NG)
        device = {"rows": row_id(lax.div(d, 2), z, lax.rem(d, 2))}
        pl.semaphore_signal(barrier, inc=1, device_id=device, device_id_type=MESH)

    pl.semaphore_signal(barrier, inc=1, device_id={"heads": 1 - t}, device_id_type=MESH)
    for load in kv_loads:
        load.start()
    w_load = pltpu.make_async_copy(w_hbm, wbuf, loc.at[2])

    def head_lanes(zz):
        return pl.ds(pl.multiple_of(zz * HEAD_DIM, HEAD_DIM), HEAD_DIM)

    chunks = 3 * len(STAGES)

    def start_chunk(ch):
        st, a = ch // 3, ch % 3
        rows = stage_cols(st)
        local(hbm[a].at[rows, head_lanes(z)], zbuf.at[a, z, rows], zrs.at[ch])

        @each_z_mate
        def _(zz, device):
            remote(hbm[a].at[rows, head_lanes(zz)], zbuf.at[a, z, rows], zss.at[ch], zrs.at[ch], device).start()

    def chunk_left(ch):
        drain(zbuf.at[ch % 3, pl.ds(0, NZ - 1), stage_cols(ch // 3)], zss.at[ch])

    lane1 = iota((1, HEAD_DIM), 1)
    sub16 = iota((SUMS, COLS), 0)
    as_row = jnp.full((1, HEAD_DIM), -1, jnp.int32)
    as_col = jnp.full((SUMS, COLS), -1, jnp.int32)
    for j in range(SUMS):
        as_row = jnp.where(lane1 == j, cols_ref[j], as_row)
        as_col = jnp.where(sub16 == j, cols_ref[j], as_col)
    pick = jnp.where(iota((SUMS, COLS), 1) == as_col, 1.0, 0.0).astype(BF)
    for a, load in enumerate(kv_loads):
        load.wait()
        ssel[a] = nn(pick, kvl[a]).astype(BF)

    pl.semaphore_wait(barrier, NZ - 1 + 2 * NG - 1 + 1)

    local(ssel.at[:, :, head_lanes(z)], sz.at[:, z], zrs.at[chunks])

    @each_z_mate
    def _(zz, device):
        remote(ssel.at[:, :, head_lanes(zz)], sz.at[:, z], zss.at[chunks], zrs.at[chunks], device).start()

    for ch in range(3):
        start_chunk(ch)
    w_load.start()

    lane = iota((COLS, HEAD_DIM), 1)
    not_own = jnp.where(iota((COLS, HEAD_DIM), 0) == as_row, -BIG, 0.0)
    for zz in range(NZ):
        pos = lane - SUMS
        kz, cc = pos % NZ, pos // NZ
        later = (kz > zz) | ((kz == zz) & (cc >= c))
        in_lanes = (pos >= 0) & (pos < 2 * NZ)
        qb[zz] = jnp.where((in_lanes & later) | (lane == 3 * SUMS), -BIG, not_own).astype(BF)
    key = iota((COLS, HEAD_DIM), 0)
    for_j = lane == key % SUMS
    for_row = lane == SUMS + key // SUMS
    ekey[0] = jnp.where(for_j, 1.0, 0.0).astype(BF)
    ekey[1] = jnp.where(for_j | for_row, 1.0, 0.0).astype(BF)
    ekey[2] = jnp.where(lane == 3 * SUMS, 1.0, 0.0).astype(BF)
    out_i, in_i = iota((COLS, COLS), 0), iota((COLS, COLS), 1)
    perm[...] = jnp.where((out_i // 16 == in_i % 16) & (out_i % 16 == in_i // 16), 1.0, 0.0).astype(BF)
    eye = jnp.where(out_i == in_i, 1.0, 0.0).astype(BF)
    eye1 = eye[:HEAD_DIM, :HEAD_DIM]
    ones = jnp.ones((16, 2 * COLS), BF)
    acc[...] = jnp.zeros_like(acc)
    mx[...] = jnp.full_like(mx, -BIG)
    tot[...] = jnp.zeros_like(tot)

    def share_summary():
        drain(sz, zrs.at[chunks])
        local(sz, sg.at[c, :, g], grs.at[0])

        @pl.loop(1, NG)
        def _(s):
            remote(sz, sg.at[c, :, g], gss.at[0], grs.at[0], {"rows": row_id(lax.rem(g + s, NG), z, c)}).start()

    def share_summary_cores():
        drain(sg.at[c], grs.at[0])
        remote(sg.at[c], sg.at[c], gss.at[1], grs.at[1], {"rows": row_id(g, z, 1 - c)}).start()

    def forward(a, st):
        ch = st * 3 + a
        drain(zbuf.at[a, :, stage_cols(st)], zrs.at[ch])
        if ch < len(NEXT):
            chunk_left(ch)
            for later in NEXT[ch]:
                start_chunk(later)
        first, count, _w = STAGES[st]

        def part(k):
            return zbuf.at[a, :, pl.ds(pl.multiple_of((first + k) * BLOCK, BLOCK), BLOCK)]

        def send(k):
            gg, cc = owner(st, k)
            remote(part(k), pbuf.at[a, p], pss.at[a, st], prs.at[a], {"rows": row_id(gg, z, cc)}).start()

        k0 = my_block(st)

        @pl.loop(1, count)
        def _(s):
            send(lax.rem(k0 + s, count))

        @pl.when(mine(st))
        def _():
            local(part(k0), pbuf.at[a, p], prs.at[a])

        @pl.when(jnp.logical_not(mine(st)))
        def _():
            send(k0)

    def update(st, i, lanes, s, vt):
        old = mx[st, i, :1, lanes]
        new = jnp.maximum(old, jnp.max(s, axis=0, keepdims=True))
        shrink = jnp.exp2(old - new)
        got = nn(vt, jnp.exp2(s - new).astype(BF))
        acc[st, i, :, lanes] = acc[st, i, :, lanes] * shrink + got[:HEAD_DIM]
        tot[st, i, :1, lanes] = tot[st, i, :1, lanes] * shrink + got[HEAD_DIM : HEAD_DIM + 1]
        mx[st, i, :1, lanes] = new

    def static_cols(st):
        return slice(STAGES[st][0] * BLOCK, STAGES[st][0] * BLOCK + STAGES[st][2])

    def summary(st, part=0, parts=1):
        per = LANES // STAGES[st][2]
        steps = lax.div(g + 2, 2)

        @pl.loop(lax.div(steps * part, parts), lax.div(steps * (part + 1), parts))
        def _(step):
            both = [(2 * step + e, cc) for e in range(2) for cc in range(2)]
            keys, vals = (
                jnp.concatenate([sg[cc, a, gg].reshape(HEAD_DIM, HEAD_DIM) for gg, cc in both], axis=0) for a in range(2)
            )
            kind = [ekey[jnp.clip(2 * step + e - g + 1, 0, 2)] for e in range(2)]
            keys = jnp.concatenate([keys, jnp.concatenate(kind, axis=0)], axis=1)
            vt = jnp.concatenate([nt(eye1, vals).astype(BF), ones], axis=0)
            for i in range(NZ // per):
                rows = slice(per * i, per * i + per)
                qs = [r.reshape(LANES, HEAD_DIM) for r in (zbuf[0, rows, static_cols(st)], qb[rows, static_cols(st)])]
                update(st, i, slice(0, LANES), nt(keys, jnp.concatenate(qs, axis=1)) * TO_LOG2, vt)

    def near(st):
        width = STAGES[st][2]
        n = STAGES[st][0] * BLOCK + width
        per = HEAD_DIM // width
        ki, qi = iota((per * n, HEAD_DIM), 0), iota((per * n, HEAD_DIM), 1)
        before = ki % n if per == 1 else jnp.where(ki >= n, ki - n, ki)
        before = before < qi % width + STAGES[st][0] * BLOCK
        if per > 1:
            before = before & ((ki >= n) == (qi >= width))

        @pl.loop(0, NZ // per // 2, unroll=NZ // per // 2)
        def _(i):
            for e in range(2):
                rows = pl.ds((2 * i + e) * per, per)
                s = nt(
                    zbuf[1, rows, :n].reshape(per * n, HEAD_DIM),
                    zbuf[0, rows, static_cols(st)].reshape(HEAD_DIM, HEAD_DIM),
                )
                s = jnp.where(before, s * TO_LOG2, -BIG)
                vt = nt(eye1, zbuf[2, rows, :n].reshape(per * n, HEAD_DIM)).astype(BF)
                vt = jnp.concatenate([vt, ones[:, : per * n]], axis=0)
                update(st, i, slice(e * HEAD_DIM, (e + 1) * HEAD_DIM), s, vt)

    sh = (HEAD_DIM, HEAD_DIM)

    def by_column(a):
        drain(pbuf.at[a], prs.at[a])

        @pl.loop(0, NG, unroll=NG)
        def _(gg):
            y = nn(perm[...], pbuf[a, pl.ds(2 * gg, 2)].reshape(COLS, HEAD_DIM))
            ybuf[a, :, gg] = y.astype(BF).reshape(BLOCK, 16, HEAD_DIM)

    def lse_lane(st, i):
        at = my_block(st) * BLOCK + i
        if STAGES[st][2] < HEAD_DIM:
            at = at + (iota(sh, 0) % 2) * STAGES[st][2]
        return iota(sh, 1) == at

    def column_weights(st):
        @pl.when(mine(st))
        def _():
            by_column(0)
            by_column(1)

            def row_of(i):
                return (i // 16) * 16 + (i % 8) * 2 + (i // 8) % 2

            causal = row_of(iota(sh, 1)) <= row_of(iota(sh, 0))
            lsrc[...] = jnp.zeros_like(lsrc)

            @pl.loop(0, BLOCK, unroll=UNROLL)
            def _(i):
                qc, kc = (ybuf[a, i].reshape(sh) for a in range(2))
                s = jnp.where(causal, nt(qc, kc) * TO_LOG2, -BIG)
                peak = jnp.max(s, axis=1, keepdims=True)
                wts[i] = jnp.exp2(s - peak).astype(BF)
                lsrc[...] = jnp.where(lse_lane(st, i), peak, lsrc[...])

    def column_values(st):
        first, count, _w = STAGES[st]

        @pl.when(mine(st))
        def _():
            by_column(2)
            one = jnp.ones(sh, BF)

            @pl.loop(0, BLOCK, unroll=UNROLL)
            def _(i):
                got = nn(wts[i], jnp.concatenate([ybuf[2, i].reshape(sh), one], axis=1))
                total = got[:, HEAD_DIM:]
                obuf[i] = (got[:, :HEAD_DIM] / total).astype(BF).reshape(NG, 16, HEAD_DIM)
                lsrc[...] = lsrc[...] + jnp.where(lse_lane(st, i), jnp.log2(total), 0.0)

            b = first + my_block(st)

            def give_back(gg):
                y = nn(perm[...], obuf[:, gg].reshape(COLS, HEAD_DIM))
                rbuf[pl.ds(2 * gg, 2)] = y.astype(BF).reshape(2, NZ, BLOCK, HEAD_DIM)

            def tile(d):
                return lsrc.at[pl.ds(pl.multiple_of(d * NZ, NZ), NZ)]

            def send_back(gg, cc):
                d = gg * 2 + cc
                device = {"rows": row_id(gg, z, cc)}
                remote(tile(d), lbuf.at[b], lss, lrs.at[st], device).start()
                remote(rbuf.at[d], cbuf.at[b], rss, rrs.at[st], device).start()

            @pl.loop(1, NG)
            def _(s):
                gg = lax.rem(g + s, NG)
                give_back(gg)
                for cc in range(2):
                    send_back(gg, cc)

            give_back(g)
            send_back(g, 1 - c)
            local(rbuf.at[p], cbuf.at[b], rrs.at[st])
            local(tile(p), lbuf.at[b], lrs.at[st])

    def merge(st):
        first, count, width = STAGES[st]
        drain(lbuf.at[pl.ds(first, count)], lrs.at[st])
        drain(cbuf.at[pl.ds(first, count)], rrs.at[st])
        lse_all = jnp.sum(lbuf[first : first + count], axis=0)
        per = LANES // width
        for i in range(NZ // per):
            rows = range(per * i, per * i + per)
            lse = [lse_all[zz : zz + 1] for zz in rows]
            if per > 2:
                lse = [lse[0] + lse[1], lse[2] + lse[3]]
            lse = jnp.concatenate(lse, axis=1)
            m = mx[st, i, :1]
            peak = jnp.maximum(m, lse)
            near_w = jnp.exp2(m - peak)
            col_w = jnp.exp2(lse - peak)
            inv = 1.0 / (tot[st, i, :1] * near_w + col_w)
            col = [cbuf[first : first + count, zz].reshape(width, HEAD_DIM) for zz in rows]
            col_t = nt(eye1, jnp.concatenate(col, axis=0))
            out_t = acc[st, i] * (near_w * inv) + col_t * (col_w * inv)
            out = nt(eye, out_t.astype(BF)).astype(BF)
            abuf[per * i : per * i + per, static_cols(st)] = out.reshape(per, width, HEAD_DIM)
        cols = stage_cols(st)
        local(abuf.at[z, cols], home.at[cols, head_lanes(z)], ars.at[st])

        @each_z_mate
        def _(zz, device):
            remote(abuf.at[zz, cols], home.at[cols, head_lanes(z)], ass.at[st], ars.at[st], device).start()

    width = NZ * HEAD_DIM

    def project(st):
        cols = stage_cols(st)
        drain(home.at[cols], ars.at[st])
        theirs = pl.ds(pl.multiple_of((1 - t) * width, width), width)
        ours = pl.ds(pl.multiple_of(t * width, width), width)
        xsend[cols] = nn(home[cols], wbuf[:, theirs]).astype(BF)
        remote(xsend.at[cols], xrecv.at[cols], xss.at[st], xrs.at[st], {"heads": 1 - t}).start()
        own[cols] = nn(home[cols], wbuf[:, ours])

    def finish(st):
        cols = stage_cols(st)
        drain(xrecv.at[cols], xrs.at[st])
        res[cols] = (own[cols] + xrecv[cols].astype(F32)).astype(BF)
        local(res.at[cols], o_ref.at[cols], loc.at[3 + st])

    Q, K, V = range(3)
    share_summary()
    forward(Q, 0)
    share_summary_cores()
    forward(K, 0)
    drain(sg.at[1 - c], grs.at[1])
    summary(0, 0, 4)
    summary(0, 1, 4)
    summary(0, 2, 4)
    forward(V, 0)
    summary(0, 3, 4)
    near(0)
    forward(Q, 1)
    column_weights(0)
    forward(K, 1)
    summary(1, 0, 2)
    column_values(0)
    forward(V, 1)
    summary(1, 1, 2)
    forward(Q, 2)
    column_weights(1)
    forward(K, 2)
    near(1)
    forward(V, 2)
    column_values(1)
    summary(2, 0, 2)
    summary(2, 1, 2)
    merge(0)
    column_weights(2)
    column_values(2)
    near(2)
    merge(1)
    w_load.wait()
    project(0)
    merge(2)
    project(1)
    project(2)
    finish(0)
    finish(1)
    finish(2)

    drain(sz.at[:, pl.ds(0, NZ - 1)], zss.at[chunks])
    drain(sg.at[0, :, pl.ds(0, NG - 1)], gss.at[0])
    drain(sg.at[c], gss.at[1])
    for ch in range(len(NEXT), chunks):
        chunk_left(ch)
    for st, (first, count, _w) in enumerate(STAGES):
        for a in range(3):

            @pl.when(mine(st))
            def _():
                drain(pbuf.at[a, pl.ds(0, count - 1)], pss.at[a, st])

            @pl.when(jnp.logical_not(mine(st)))
            def _():
                drain(pbuf.at[a, pl.ds(0, count)], pss.at[a, st])

        cols = stage_cols(st)
        drain(abuf.at[pl.ds(0, NZ - 1), cols], ass.at[st])
        drain(xsend.at[cols], xss.at[st])
        pltpu.make_async_copy(res.at[cols], o_ref.at[cols], loc.at[3 + st]).wait()
    drain(rbuf.at[pl.ds(0, 2 * NG - 1)], rss)
    drain(lsrc.at[pl.ds(0, (2 * NG - 1) * NZ)], lss)


def on_device(queries, keys, values, summary_cols, w_out):
    width = queries.shape[1]
    any_space = pl.BlockSpec(memory_space=pl.ANY)
    dma = pltpu.SemaphoreType.DMA
    vmem = pltpu.VMEM
    e = HEAD_DIM
    n = len(STAGES)
    return pl.pallas_call(
        body,
        out_shape=jax.ShapeDtypeStruct(queries.shape, BF),
        in_specs=[pl.BlockSpec(memory_space=pltpu.SMEM)] + [any_space] * 4,
        out_specs=any_space,
        scratch_shapes=[
            vmem((3, NZ, COLS, e), BF),
            vmem((3, 2 * NG, NZ, BLOCK, e), BF),
            vmem((3, BLOCK, NG, 16, e), BF),
            vmem((BLOCK, e, e), BF),
            vmem((BLOCK, NG, 16, e), BF),
            vmem((2 * NG, NZ, BLOCK, e), BF),
            vmem((2 * NG, NZ, BLOCK, e), BF),
            vmem((NZ, COLS, e), BF),
            vmem((COLS, width), BF),
            vmem(w_out.shape, BF),
            vmem((2, COLS, width), BF),
            vmem((2, SUMS, width), BF),
            vmem((2, NZ, SUMS, e), BF),
            vmem((2, 2, NG, NZ, SUMS, e), BF),
            vmem((NZ, COLS, e), BF),
            vmem((3, COLS, e), BF),
            vmem((COLS, COLS), BF),
            vmem((e, e), F32),
            vmem((2 * NG, NZ, e), F32),
            vmem((n, NZ // 2, e, LANES), F32),
            vmem((n, NZ // 2, 8, LANES), F32),
            vmem((n, NZ // 2, 8, LANES), F32),
            vmem((COLS, width), F32),
            vmem((COLS, width), BF),
            vmem((COLS, width), BF),
            vmem((COLS, width), BF),
            dma((3 * n + 1,)), dma((3 * n + 1,)),
            dma((2,)), dma((2,)),
            dma((3, n)), dma((3,)),
            dma, dma((n,)),
            dma, dma((n,)),
            dma((n,)), dma((n,)),
            dma((n,)), dma((n,)),
            dma((3 + n,)),
        ],
        name="strided_attention",
        compiler_params=pltpu.CompilerParams(
            collective_id=0, has_side_effects=True, vmem_limit_bytes=53 * 1024 * 1024
        ),
    )(summary_cols, queries, keys, values, w_out)


def solution(mesh):
    return jax.shard_map(
        on_device,
        mesh=mesh,
        in_specs=(P("rows", "heads"), P("rows", "heads"), P("rows", "heads"), P(), P("heads", None)),
        out_specs=P("rows", "heads"),
        check_vma=False,
    )
```

```python
import math

import jax
import jax.numpy as jnp
from jax import lax
from jax.experimental import pallas as pl
from jax.experimental.pallas import tpu as pltpu
from jax.sharding import PartitionSpec as P

HEAD_DIM = 128
COLS = 256
SUMS = 16
NZ = 8
NG = 8
BLOCK = 16
LANES = 256
STAGES = ((0, 8, 128), (8, 4, 64), (12, 4, 64))
UNROLL = 16
NEXT = ((3,), (4,), (5,), (6,), (7,), (8,))
MESH = pl.DeviceIdType.MESH
BF, F32 = jnp.bfloat16, jnp.float32
BIG = 1e30
TO_LOG2 = math.log2(math.e) / math.sqrt(HEAD_DIM)


def nt(a, b):
    return lax.dot_general(a, b, (((1,), (1,)), ((), ())), preferred_element_type=F32)


def nn(a, b):
    return jnp.dot(a, b, preferred_element_type=F32)


def iota(shape, dim):
    return lax.broadcasted_iota(jnp.int32, shape, dim)


def body(cols_ref, q_hbm, k_hbm, v_hbm, w_hbm, o_ref, zbuf, pbuf, ybuf, wts, obuf, rbuf, cbuf, abuf, home, wbuf,
         kvl, ssel, sz, sg, qb, ekey, perm, lsrc, lbuf, acc, mx, tot, own, xsend, xrecv, res,
         zss, zrs, gss, grs, pss, prs, rss, rrs, lss, lrs, ass, ars, xss, xrs, loc):
    me = lax.axis_index("rows")
    t = lax.axis_index("heads")
    c = lax.rem(me, 2)
    z = lax.rem(lax.div(me, 2), NZ)
    g = lax.div(me, 2 * NZ)
    p = g * 2 + c
    x, y_hi = lax.div(g, 2), lax.rem(g, 2)
    odd_x = lax.rem(x, 2)

    def row_id(gg, zz, cc):
        return (gg * NZ + zz) * 2 + cc

    def z_mate(s):
        zz = lax.rem(z + s, NZ)
        return zz, {"rows": row_id(g, zz, c)}

    def each_z_mate(act):
        @pl.loop(1, NZ // 2)
        def _(s):
            act(*z_mate(s))
            act(*z_mate(NZ - s))

        act(*z_mate(NZ // 2))

    def remote(src, dst, ssem, rsem, device):
        return pltpu.make_async_remote_copy(
            src_ref=src, dst_ref=dst, send_sem=ssem, recv_sem=rsem, device_id=device, device_id_type=MESH
        )

    def local(src, dst, sem):
        pltpu.make_async_copy(src, dst, sem).start()

    def drain(ref, sem):
        pltpu.make_async_copy(ref, ref, sem).wait()

    def owner(st, k):
        if st == 0:
            return k, 0
        return 4 * lax.div(k, 2) + 2 * (st - 1) + lax.rem(k, 2), 1

    def mine(st):
        if st == 0:
            return c == 0
        return (c == 1) & (odd_x == st - 1)

    def my_block(st):
        return g if st == 0 else 2 * lax.div(x, 2) + y_hi

    def stage_cols(st):
        return pl.ds(STAGES[st][0] * BLOCK, STAGES[st][2])

    hbm = (q_hbm, k_hbm, v_hbm)
    kv_loads = [pltpu.make_async_copy(hbm[1 + a], kvl.at[a], loc.at[a]) for a in range(2)]
    barrier = pltpu.get_barrier_semaphore()

    @pl.loop(1, NZ)
    def _(s):
        pl.semaphore_signal(barrier, inc=1, device_id=z_mate(s)[1], device_id_type=MESH)

    @pl.loop(1, 2 * NG)
    def _(s):
        d = lax.rem(p + s, 2 * NG)
        device = {"rows": row_id(lax.div(d, 2), z, lax.rem(d, 2))}
        pl.semaphore_signal(barrier, inc=1, device_id=device, device_id_type=MESH)

    pl.semaphore_signal(barrier, inc=1, device_id={"heads": 1 - t}, device_id_type=MESH)
    for load in kv_loads:
        load.start()
    w_load = pltpu.make_async_copy(w_hbm, wbuf, loc.at[2])

    def head_lanes(zz):
        return pl.ds(pl.multiple_of(zz * HEAD_DIM, HEAD_DIM), HEAD_DIM)

    chunks = 3 * len(STAGES)

    def start_chunk(ch):
        st, a = ch // 3, ch % 3
        rows = stage_cols(st)
        local(hbm[a].at[rows, head_lanes(z)], zbuf.at[a, z, rows], zrs.at[ch])

        @each_z_mate
        def _(zz, device):
            remote(hbm[a].at[rows, head_lanes(zz)], zbuf.at[a, z, rows], zss.at[ch], zrs.at[ch], device).start()

    def chunk_left(ch):
        drain(zbuf.at[ch % 3, pl.ds(0, NZ - 1), stage_cols(ch // 3)], zss.at[ch])

    lane1 = iota((1, HEAD_DIM), 1)
    sub16 = iota((SUMS, COLS), 0)
    as_row = jnp.full((1, HEAD_DIM), -1, jnp.int32)
    as_col = jnp.full((SUMS, COLS), -1, jnp.int32)
    for j in range(SUMS):
        as_row = jnp.where(lane1 == j, cols_ref[j], as_row)
        as_col = jnp.where(sub16 == j, cols_ref[j], as_col)
    pick = jnp.where(iota((SUMS, COLS), 1) == as_col, 1.0, 0.0).astype(BF)
    for a, load in enumerate(kv_loads):
        load.wait()
        ssel[a] = nn(pick, kvl[a]).astype(BF)

    pl.semaphore_wait(barrier, NZ - 1 + 2 * NG - 1 + 1)

    local(ssel.at[:, :, head_lanes(z)], sz.at[:, z], zrs.at[chunks])

    @each_z_mate
    def _(zz, device):
        remote(ssel.at[:, :, head_lanes(zz)], sz.at[:, z], zss.at[chunks], zrs.at[chunks], device).start()

    for ch in range(3):
        start_chunk(ch)
    w_load.start()

    lane = iota((COLS, HEAD_DIM), 1)
    not_own = jnp.where(iota((COLS, HEAD_DIM), 0) == as_row, -BIG, 0.0)
    for zz in range(NZ):
        pos = lane - SUMS
        kz, cc = pos % NZ, pos // NZ
        later = (kz > zz) | ((kz == zz) & (cc >= c))
        in_lanes = (pos >= 0) & (pos < 2 * NZ)
        qb[zz] = jnp.where((in_lanes & later) | (lane == 3 * SUMS), -BIG, not_own).astype(BF)
    key = iota((COLS, HEAD_DIM), 0)
    for_j = lane == key % SUMS
    for_row = lane == SUMS + key // SUMS
    ekey[0] = jnp.where(for_j, 1.0, 0.0).astype(BF)
    ekey[1] = jnp.where(for_j | for_row, 1.0, 0.0).astype(BF)
    ekey[2] = jnp.where(lane == 3 * SUMS, 1.0, 0.0).astype(BF)
    out_i, in_i = iota((COLS, COLS), 0), iota((COLS, COLS), 1)
    perm[...] = jnp.where((out_i // 16 == in_i % 16) & (out_i % 16 == in_i // 16), 1.0, 0.0).astype(BF)
    eye = jnp.where(out_i == in_i, 1.0, 0.0).astype(BF)
    eye1 = eye[:HEAD_DIM, :HEAD_DIM]
    ones = jnp.ones((16, 2 * COLS), BF)
    acc[...] = jnp.zeros_like(acc)
    mx[...] = jnp.full_like(mx, -BIG)
    tot[...] = jnp.zeros_like(tot)

    def share_summary():
        drain(sz, zrs.at[chunks])
        local(sz, sg.at[c, :, g], grs.at[0])

        @pl.loop(1, NG)
        def _(s):
            remote(sz, sg.at[c, :, g], gss.at[0], grs.at[0], {"rows": row_id(lax.rem(g + s, NG), z, c)}).start()

    def share_summary_cores():
        drain(sg.at[c], grs.at[0])
        remote(sg.at[c], sg.at[c], gss.at[1], grs.at[1], {"rows": row_id(g, z, 1 - c)}).start()

    def forward(a, st):
        ch = st * 3 + a
        drain(zbuf.at[a, :, stage_cols(st)], zrs.at[ch])
        first, count, _w = STAGES[st]

        def part(k):
            return zbuf.at[a, :, pl.ds(pl.multiple_of((first + k) * BLOCK, BLOCK), BLOCK)]

        def send(k):
            gg, cc = owner(st, k)
            remote(part(k), pbuf.at[a, p], pss.at[a, st], prs.at[a], {"rows": row_id(gg, z, cc)}).start()

        k0 = my_block(st)

        @pl.loop(1, count)
        def _(s):
            send(lax.rem(k0 + s, count))

        @pl.when(mine(st))
        def _():
            local(part(k0), pbuf.at[a, p], prs.at[a])

        @pl.when(jnp.logical_not(mine(st)))
        def _():
            send(k0)

        if ch < len(NEXT):
            chunk_left(ch)
            for later in NEXT[ch]:
                start_chunk(later)

    def update(st, i, lanes, s, vt):
        old = mx[st, i, :1, lanes]
        new = jnp.maximum(old, jnp.max(s, axis=0, keepdims=True))
        shrink = jnp.exp2(old - new)
        got = nn(vt, jnp.exp2(s - new).astype(BF))
        acc[st, i, :, lanes] = acc[st, i, :, lanes] * shrink + got[:HEAD_DIM]
        tot[st, i, :1, lanes] = tot[st, i, :1, lanes] * shrink + got[HEAD_DIM : HEAD_DIM + 1]
        mx[st, i, :1, lanes] = new

    def static_cols(st):
        return slice(STAGES[st][0] * BLOCK, STAGES[st][0] * BLOCK + STAGES[st][2])

    def summary(st, part=0, parts=1):
        per = LANES // STAGES[st][2]
        steps = lax.div(g + 2, 2)

        @pl.loop(lax.div(steps * part, parts), lax.div(steps * (part + 1), parts))
        def _(step):
            both = [(2 * step + e, cc) for e in range(2) for cc in range(2)]
            keys, vals = (
                jnp.concatenate([sg[cc, a, gg].reshape(HEAD_DIM, HEAD_DIM) for gg, cc in both], axis=0) for a in range(2)
            )
            kind = [ekey[jnp.clip(2 * step + e - g + 1, 0, 2)] for e in range(2)]
            keys = jnp.concatenate([keys, jnp.concatenate(kind, axis=0)], axis=1)
            vt = jnp.concatenate([nt(eye1, vals).astype(BF), ones], axis=0)
            for i in range(NZ // per):
                rows = slice(per * i, per * i + per)
                qs = [r.reshape(LANES, HEAD_DIM) for r in (zbuf[0, rows, static_cols(st)], qb[rows, static_cols(st)])]
                update(st, i, slice(0, LANES), nt(keys, jnp.concatenate(qs, axis=1)) * TO_LOG2, vt)

    def near(st):
        width = STAGES[st][2]
        n = STAGES[st][0] * BLOCK + width
        per = HEAD_DIM // width
        ki, qi = iota((per * n, HEAD_DIM), 0), iota((per * n, HEAD_DIM), 1)
        before = ki % n if per == 1 else jnp.where(ki >= n, ki - n, ki)
        before = before < qi % width + STAGES[st][0] * BLOCK
        if per > 1:
            before = before & ((ki >= n) == (qi >= width))

        @pl.loop(0, NZ // per // 2, unroll=NZ // per // 2)
        def _(i):
            for e in range(2):
                rows = pl.ds((2 * i + e) * per, per)
                s = nt(
                    zbuf[1, rows, :n].reshape(per * n, HEAD_DIM),
                    zbuf[0, rows, static_cols(st)].reshape(HEAD_DIM, HEAD_DIM),
                )
                s = jnp.where(before, s * TO_LOG2, -BIG)
                vt = nt(eye1, zbuf[2, rows, :n].reshape(per * n, HEAD_DIM)).astype(BF)
                vt = jnp.concatenate([vt, ones[:, : per * n]], axis=0)
                update(st, i, slice(e * HEAD_DIM, (e + 1) * HEAD_DIM), s, vt)

    sh = (HEAD_DIM, HEAD_DIM)

    def by_column(a):
        drain(pbuf.at[a], prs.at[a])

        @pl.loop(0, NG, unroll=NG)
        def _(gg):
            y = nn(perm[...], pbuf[a, pl.ds(2 * gg, 2)].reshape(COLS, HEAD_DIM))
            ybuf[a, :, gg] = y.astype(BF).reshape(BLOCK, 16, HEAD_DIM)

    def lse_lane(st, i):
        at = my_block(st) * BLOCK + i
        if STAGES[st][2] < HEAD_DIM:
            at = at + (iota(sh, 0) % 2) * STAGES[st][2]
        return iota(sh, 1) == at

    def column_weights(st):
        @pl.when(mine(st))
        def _():
            by_column(0)
            by_column(1)

            def row_of(i):
                return (i // 16) * 16 + (i % 8) * 2 + (i // 8) % 2

            causal = row_of(iota(sh, 1)) <= row_of(iota(sh, 0))
            lsrc[...] = jnp.zeros_like(lsrc)

            @pl.loop(0, BLOCK, unroll=UNROLL)
            def _(i):
                qc, kc = (ybuf[a, i].reshape(sh) for a in range(2))
                s = jnp.where(causal, nt(qc, kc) * TO_LOG2, -BIG)
                peak = jnp.max(s, axis=1, keepdims=True)
                wts[i] = jnp.exp2(s - peak).astype(BF)
                lsrc[...] = jnp.where(lse_lane(st, i), peak, lsrc[...])

    def column_values(st):
        first, count, _w = STAGES[st]

        @pl.when(mine(st))
        def _():
            by_column(2)
            one = jnp.ones(sh, BF)

            @pl.loop(0, BLOCK, unroll=UNROLL)
            def _(i):
                got = nn(wts[i], jnp.concatenate([ybuf[2, i].reshape(sh), one], axis=1))
                total = got[:, HEAD_DIM:]
                obuf[i] = (got[:, :HEAD_DIM] / total).astype(BF).reshape(NG, 16, HEAD_DIM)
                lsrc[...] = lsrc[...] + jnp.where(lse_lane(st, i), jnp.log2(total), 0.0)

            b = first + my_block(st)

            def give_back(gg):
                y = nn(perm[...], obuf[:, gg].reshape(COLS, HEAD_DIM))
                rbuf[2 * gg : 2 * gg + 2] = y.astype(BF).reshape(2, NZ, BLOCK, HEAD_DIM)

            def tile(d):
                return lsrc.at[pl.ds(pl.multiple_of(d * NZ, NZ), NZ)]

            def send_back(gg, cc):
                d = gg * 2 + cc
                device = {"rows": row_id(gg, z, cc)}
                remote(tile(d), lbuf.at[b], lss, lrs.at[st], device).start()
                remote(rbuf.at[d], cbuf.at[b], rss, rrs.at[st], device).start()

            for gg in range(NG):
                give_back(gg)

            @pl.loop(1, NG)
            def _(s):
                gg = lax.rem(g + s, NG)
                for cc in range(2):
                    send_back(gg, cc)

            send_back(g, 1 - c)
            local(rbuf.at[p], cbuf.at[b], rrs.at[st])
            local(tile(p), lbuf.at[b], lrs.at[st])

    def merge(st):
        first, count, width = STAGES[st]
        drain(lbuf.at[pl.ds(first, count)], lrs.at[st])
        drain(cbuf.at[pl.ds(first, count)], rrs.at[st])
        lse_all = jnp.sum(lbuf[first : first + count], axis=0)
        per = LANES // width
        for i in range(NZ // per):
            rows = range(per * i, per * i + per)
            lse = [lse_all[zz : zz + 1] for zz in rows]
            if per > 2:
                lse = [lse[0] + lse[1], lse[2] + lse[3]]
            lse = jnp.concatenate(lse, axis=1)
            m = mx[st, i, :1]
            peak = jnp.maximum(m, lse)
            near_w = jnp.exp2(m - peak)
            col_w = jnp.exp2(lse - peak)
            inv = 1.0 / (tot[st, i, :1] * near_w + col_w)
            col = [cbuf[first : first + count, zz].reshape(width, HEAD_DIM) for zz in rows]
            col_t = nt(eye1, jnp.concatenate(col, axis=0))
            out_t = acc[st, i] * (near_w * inv) + col_t * (col_w * inv)
            out = nt(eye, out_t.astype(BF)).astype(BF)
            abuf[per * i : per * i + per, static_cols(st)] = out.reshape(per, width, HEAD_DIM)
        cols = stage_cols(st)
        local(abuf.at[z, cols], home.at[cols, head_lanes(z)], ars.at[st])

        @each_z_mate
        def _(zz, device):
            remote(abuf.at[zz, cols], home.at[cols, head_lanes(z)], ass.at[st], ars.at[st], device).start()

    width = NZ * HEAD_DIM

    def project(st):
        cols = stage_cols(st)
        drain(home.at[cols], ars.at[st])
        theirs = pl.ds(pl.multiple_of((1 - t) * width, width), width)
        ours = pl.ds(pl.multiple_of(t * width, width), width)
        xsend[cols] = nn(home[cols], wbuf[:, theirs]).astype(BF)
        remote(xsend.at[cols], xrecv.at[cols], xss.at[st], xrs.at[st], {"heads": 1 - t}).start()
        own[cols] = nn(home[cols], wbuf[:, ours])

    def finish(st):
        cols = stage_cols(st)
        drain(xrecv.at[cols], xrs.at[st])
        res[cols] = (own[cols] + xrecv[cols].astype(F32)).astype(BF)
        local(res.at[cols], o_ref.at[cols], loc.at[3 + st])

    Q, K, V = range(3)
    share_summary()
    forward(Q, 0)
    share_summary_cores()
    forward(K, 0)
    drain(sg.at[1 - c], grs.at[1])
    summary(0, 0, 4)
    summary(0, 1, 4)
    summary(0, 2, 4)
    forward(V, 0)
    summary(0, 3, 4)
    near(0)
    forward(Q, 1)
    column_weights(0)
    forward(K, 1)
    summary(1, 0, 2)
    column_values(0)
    forward(V, 1)
    summary(1, 1, 2)
    forward(Q, 2)
    forward(K, 2)
    column_weights(1)
    near(1)
    forward(V, 2)
    column_values(1)
    summary(2, 0, 2)
    merge(0)
    summary(2, 1, 2)
    column_weights(2)
    column_values(2)
    near(2)
    merge(1)
    w_load.wait()
    project(0)
    merge(2)
    project(1)
    project(2)
    finish(0)
    finish(1)
    finish(2)

    drain(sz.at[:, pl.ds(0, NZ - 1)], zss.at[chunks])
    drain(sg.at[0, :, pl.ds(0, NG - 1)], gss.at[0])
    drain(sg.at[c], gss.at[1])
    for ch in range(len(NEXT), chunks):
        chunk_left(ch)
    for st, (first, count, _w) in enumerate(STAGES):
        for a in range(3):

            @pl.when(mine(st))
            def _():
                drain(pbuf.at[a, pl.ds(0, count - 1)], pss.at[a, st])

            @pl.when(jnp.logical_not(mine(st)))
            def _():
                drain(pbuf.at[a, pl.ds(0, count)], pss.at[a, st])

        cols = stage_cols(st)
        drain(abuf.at[pl.ds(0, NZ - 1), cols], ass.at[st])
        drain(xsend.at[cols], xss.at[st])
        pltpu.make_async_copy(res.at[cols], o_ref.at[cols], loc.at[3 + st]).wait()
    drain(rbuf.at[pl.ds(0, 2 * NG - 1)], rss)
    drain(lsrc.at[pl.ds(0, (2 * NG - 1) * NZ)], lss)


def on_device(queries, keys, values, summary_cols, w_out):
    width = queries.shape[1]
    any_space = pl.BlockSpec(memory_space=pl.ANY)
    dma = pltpu.SemaphoreType.DMA
    vmem = pltpu.VMEM
    e = HEAD_DIM
    n = len(STAGES)
    return pl.pallas_call(
        body,
        out_shape=jax.ShapeDtypeStruct(queries.shape, BF),
        in_specs=[pl.BlockSpec(memory_space=pltpu.SMEM)] + [any_space] * 4,
        out_specs=any_space,
        scratch_shapes=[
            vmem((3, NZ, COLS, e), BF),
            vmem((3, 2 * NG, NZ, BLOCK, e), BF),
            vmem((3, BLOCK, NG, 16, e), BF),
            vmem((BLOCK, e, e), BF),
            vmem((BLOCK, NG, 16, e), BF),
            vmem((2 * NG, NZ, BLOCK, e), BF),
            vmem((2 * NG, NZ, BLOCK, e), BF),
            vmem((NZ, COLS, e), BF),
            vmem((COLS, width), BF),
            vmem(w_out.shape, BF),
            vmem((2, COLS, width), BF),
            vmem((2, SUMS, width), BF),
            vmem((2, NZ, SUMS, e), BF),
            vmem((2, 2, NG, NZ, SUMS, e), BF),
            vmem((NZ, COLS, e), BF),
            vmem((3, COLS, e), BF),
            vmem((COLS, COLS), BF),
            vmem((e, e), F32),
            vmem((2 * NG, NZ, e), F32),
            vmem((n, NZ // 2, e, LANES), F32),
            vmem((n, NZ // 2, 8, LANES), F32),
            vmem((n, NZ // 2, 8, LANES), F32),
            vmem((COLS, width), F32),
            vmem((COLS, width), BF),
            vmem((COLS, width), BF),
            vmem((COLS, width), BF),
            dma((3 * n + 1,)), dma((3 * n + 1,)),
            dma((2,)), dma((2,)),
            dma((3, n)), dma((3,)),
            dma, dma((n,)),
            dma, dma((n,)),
            dma((n,)), dma((n,)),
            dma((n,)), dma((n,)),
            dma((3 + n,)),
        ],
        name="strided_attention",
        compiler_params=pltpu.CompilerParams(
            collective_id=0, has_side_effects=True, vmem_limit_bytes=53 * 1024 * 1024
        ),
    )(summary_cols, queries, keys, values, w_out)


def solution(mesh):
    return jax.shard_map(
        on_device,
        mesh=mesh,
        in_specs=(P("rows", "heads"), P("rows", "heads"), P("rows", "heads"), P(), P("heads", None)),
        out_specs=P("rows", "heads"),
        check_vma=False,
    )
```

```python
import math

import jax
import jax.numpy as jnp
from jax import lax
from jax.experimental import pallas as pl
from jax.experimental.pallas import tpu as pltpu
from jax.sharding import PartitionSpec as P

HEAD_DIM = 128
COLS = 256
SUMS = 16
NZ = 8
NG = 8
BLOCK = 16
LANES = 256
STAGES = ((0, 8, 128), (8, 4, 64), (12, 4, 64))
UNROLL = 16
NEXT = ((3,), (4,), (5,), (6,), (7,), (8,))
MESH = pl.DeviceIdType.MESH
BF, F32 = jnp.bfloat16, jnp.float32
BIG = 1e30
TO_LOG2 = math.log2(math.e) / math.sqrt(HEAD_DIM)


def nt(a, b):
    return lax.dot_general(a, b, (((1,), (1,)), ((), ())), preferred_element_type=F32)


def nn(a, b):
    return jnp.dot(a, b, preferred_element_type=F32)


def iota(shape, dim):
    return lax.broadcasted_iota(jnp.int32, shape, dim)


def body(cols_ref, q_hbm, k_hbm, v_hbm, w_hbm, o_ref, zbuf, pbuf, ybuf, wts, obuf, rbuf, cbuf, abuf, home, wbuf,
         kvl, ssel, sz, sg, qb, ekey, perm, lsrc, lbuf, acc, mx, tot, own, xsend, xrecv, res,
         zss, zrs, gss, grs, pss, prs, rss, rrs, lss, lrs, ass, ars, xss, xrs, loc):
    me = lax.axis_index("rows")
    t = lax.axis_index("heads")
    c = lax.rem(me, 2)
    z = lax.rem(lax.div(me, 2), NZ)
    g = lax.div(me, 2 * NZ)
    p = g * 2 + c
    x, y_hi = lax.div(g, 2), lax.rem(g, 2)
    odd_x = lax.rem(x, 2)

    def row_id(gg, zz, cc):
        return (gg * NZ + zz) * 2 + cc

    def z_mate(s):
        zz = lax.rem(z + s, NZ)
        return zz, {"rows": row_id(g, zz, c)}

    def each_z_mate(act):
        @pl.loop(1, NZ // 2)
        def _(s):
            act(*z_mate(s))
            act(*z_mate(NZ - s))

        act(*z_mate(NZ // 2))

    def remote(src, dst, ssem, rsem, device):
        return pltpu.make_async_remote_copy(
            src_ref=src, dst_ref=dst, send_sem=ssem, recv_sem=rsem, device_id=device, device_id_type=MESH
        )

    def local(src, dst, sem):
        pltpu.make_async_copy(src, dst, sem).start()

    def drain(ref, sem):
        pltpu.make_async_copy(ref, ref, sem).wait()

    def owner(st, k):
        if st == 0:
            return k, 0
        return 4 * lax.div(k, 2) + 2 * (st - 1) + lax.rem(k, 2), 1

    def mine(st):
        if st == 0:
            return c == 0
        return (c == 1) & (odd_x == st - 1)

    def my_block(st):
        return g if st == 0 else 2 * lax.div(x, 2) + y_hi

    def stage_cols(st):
        return pl.ds(STAGES[st][0] * BLOCK, STAGES[st][2])

    hbm = (q_hbm, k_hbm, v_hbm)
    kv_loads = [pltpu.make_async_copy(hbm[1 + a], kvl.at[a], loc.at[a]) for a in range(2)]
    barrier = pltpu.get_barrier_semaphore()

    @pl.loop(1, NZ)
    def _(s):
        pl.semaphore_signal(barrier, inc=1, device_id=z_mate(s)[1], device_id_type=MESH)

    @pl.loop(1, 2 * NG)
    def _(s):
        d = lax.rem(p + s, 2 * NG)
        device = {"rows": row_id(lax.div(d, 2), z, lax.rem(d, 2))}
        pl.semaphore_signal(barrier, inc=1, device_id=device, device_id_type=MESH)

    pl.semaphore_signal(barrier, inc=1, device_id={"heads": 1 - t}, device_id_type=MESH)
    for load in kv_loads:
        load.start()
    w_load = pltpu.make_async_copy(w_hbm, wbuf, loc.at[2])

    def head_lanes(zz):
        return pl.ds(pl.multiple_of(zz * HEAD_DIM, HEAD_DIM), HEAD_DIM)

    chunks = 3 * len(STAGES)

    def start_chunk(ch):
        st, a = ch // 3, ch % 3
        rows = stage_cols(st)
        local(hbm[a].at[rows, head_lanes(z)], zbuf.at[a, z, rows], zrs.at[ch])

        @each_z_mate
        def _(zz, device):
            remote(hbm[a].at[rows, head_lanes(zz)], zbuf.at[a, z, rows], zss.at[ch], zrs.at[ch], device).start()

    def chunk_left(ch):
        drain(zbuf.at[ch % 3, pl.ds(0, NZ - 1), stage_cols(ch // 3)], zss.at[ch])

    lane1 = iota((1, HEAD_DIM), 1)
    sub16 = iota((SUMS, COLS), 0)
    as_row = jnp.full((1, HEAD_DIM), -1, jnp.int32)
    as_col = jnp.full((SUMS, COLS), -1, jnp.int32)
    for j in range(SUMS):
        as_row = jnp.where(lane1 == j, cols_ref[j], as_row)
        as_col = jnp.where(sub16 == j, cols_ref[j], as_col)
    pick = jnp.where(iota((SUMS, COLS), 1) == as_col, 1.0, 0.0).astype(BF)
    for a, load in enumerate(kv_loads):
        load.wait()
        ssel[a] = nn(pick, kvl[a]).astype(BF)

    pl.semaphore_wait(barrier, NZ - 1 + 2 * NG - 1 + 1)

    local(ssel.at[:, :, head_lanes(z)], sz.at[:, z], zrs.at[chunks])

    @each_z_mate
    def _(zz, device):
        remote(ssel.at[:, :, head_lanes(zz)], sz.at[:, z], zss.at[chunks], zrs.at[chunks], device).start()

    for ch in range(3):
        start_chunk(ch)
    w_load.start()

    lane = iota((COLS, HEAD_DIM), 1)
    not_own = jnp.where(iota((COLS, HEAD_DIM), 0) == as_row, -BIG, 0.0)
    for zz in range(NZ):
        pos = lane - SUMS
        kz, cc = pos % NZ, pos // NZ
        later = (kz > zz) | ((kz == zz) & (cc >= c))
        in_lanes = (pos >= 0) & (pos < 2 * NZ)
        qb[zz] = jnp.where((in_lanes & later) | (lane == 3 * SUMS), -BIG, not_own).astype(BF)
    key = iota((COLS, HEAD_DIM), 0)
    for_j = lane == key % SUMS
    for_row = lane == SUMS + key // SUMS
    ekey[0] = jnp.where(for_j, 1.0, 0.0).astype(BF)
    ekey[1] = jnp.where(for_j | for_row, 1.0, 0.0).astype(BF)
    ekey[2] = jnp.where(lane == 3 * SUMS, 1.0, 0.0).astype(BF)
    out_i, in_i = iota((COLS, COLS), 0), iota((COLS, COLS), 1)
    perm[...] = jnp.where((out_i // 16 == in_i % 16) & (out_i % 16 == in_i // 16), 1.0, 0.0).astype(BF)
    eye = jnp.where(out_i == in_i, 1.0, 0.0).astype(BF)
    eye1 = eye[:HEAD_DIM, :HEAD_DIM]
    ones = jnp.ones((16, 2 * COLS), BF)
    acc[...] = jnp.zeros_like(acc)
    mx[...] = jnp.full_like(mx, -BIG)
    tot[...] = jnp.zeros_like(tot)

    def share_summary():
        drain(sz, zrs.at[chunks])
        local(sz, sg.at[c, :, g], grs.at[0])

        @pl.loop(1, NG)
        def _(s):
            remote(sz, sg.at[c, :, g], gss.at[0], grs.at[0], {"rows": row_id(lax.rem(g + s, NG), z, c)}).start()

    def share_summary_cores():
        drain(sg.at[c], grs.at[0])
        remote(sg.at[c], sg.at[c], gss.at[1], grs.at[1], {"rows": row_id(g, z, 1 - c)}).start()

    def forward(a, st):
        ch = st * 3 + a
        drain(zbuf.at[a, :, stage_cols(st)], zrs.at[ch])
        first, count, _w = STAGES[st]

        def part(k):
            return zbuf.at[a, :, pl.ds(pl.multiple_of((first + k) * BLOCK, BLOCK), BLOCK)]

        def send(k):
            gg, cc = owner(st, k)
            remote(part(k), pbuf.at[a, p], pss.at[a, st], prs.at[a], {"rows": row_id(gg, z, cc)}).start()

        k0 = my_block(st)

        @pl.loop(1, count)
        def _(s):
            send(lax.rem(k0 + s, count))

        @pl.when(mine(st))
        def _():
            local(part(k0), pbuf.at[a, p], prs.at[a])

        @pl.when(jnp.logical_not(mine(st)))
        def _():
            send(k0)

        if ch < len(NEXT):
            chunk_left(ch)
            for later in NEXT[ch]:
                start_chunk(later)

    def update(st, i, lanes, s, vt):
        old = mx[st, i, :1, lanes]
        new = jnp.maximum(old, jnp.max(s, axis=0, keepdims=True))
        shrink = jnp.exp2(old - new)
        got = nn(vt, jnp.exp2(s - new).astype(BF))
        acc[st, i, :, lanes] = acc[st, i, :, lanes] * shrink + got[:HEAD_DIM]
        tot[st, i, :1, lanes] = tot[st, i, :1, lanes] * shrink + got[HEAD_DIM : HEAD_DIM + 1]
        mx[st, i, :1, lanes] = new

    def static_cols(st):
        return slice(STAGES[st][0] * BLOCK, STAGES[st][0] * BLOCK + STAGES[st][2])

    def summary(st, part=0, parts=1):
        per = LANES // STAGES[st][2]
        steps = lax.div(g + 2, 2)

        @pl.loop(lax.div(steps * part, parts), lax.div(steps * (part + 1), parts))
        def _(step):
            both = [(2 * step + e, cc) for e in range(2) for cc in range(2)]
            keys, vals = (
                jnp.concatenate([sg[cc, a, gg].reshape(HEAD_DIM, HEAD_DIM) for gg, cc in both], axis=0) for a in range(2)
            )
            kind = [ekey[jnp.clip(2 * step + e - g + 1, 0, 2)] for e in range(2)]
            keys = jnp.concatenate([keys, jnp.concatenate(kind, axis=0)], axis=1)
            vt = jnp.concatenate([nt(eye1, vals).astype(BF), ones], axis=0)
            for i in range(NZ // per):
                rows = slice(per * i, per * i + per)
                qs = [r.reshape(LANES, HEAD_DIM) for r in (zbuf[0, rows, static_cols(st)], qb[rows, static_cols(st)])]
                update(st, i, slice(0, LANES), nt(keys, jnp.concatenate(qs, axis=1)) * TO_LOG2, vt)

    def near(st):
        width = STAGES[st][2]
        n = STAGES[st][0] * BLOCK + width
        per = HEAD_DIM // width
        ki, qi = iota((per * n, HEAD_DIM), 0), iota((per * n, HEAD_DIM), 1)
        before = ki % n if per == 1 else jnp.where(ki >= n, ki - n, ki)
        before = before < qi % width + STAGES[st][0] * BLOCK
        if per > 1:
            before = before & ((ki >= n) == (qi >= width))

        @pl.loop(0, NZ // per // 2, unroll=NZ // per // 2)
        def _(i):
            for e in range(2):
                rows = pl.ds((2 * i + e) * per, per)
                s = nt(
                    zbuf[1, rows, :n].reshape(per * n, HEAD_DIM),
                    zbuf[0, rows, static_cols(st)].reshape(HEAD_DIM, HEAD_DIM),
                )
                s = jnp.where(before, s * TO_LOG2, -BIG)
                vt = nt(eye1, zbuf[2, rows, :n].reshape(per * n, HEAD_DIM)).astype(BF)
                vt = jnp.concatenate([vt, ones[:, : per * n]], axis=0)
                update(st, i, slice(e * HEAD_DIM, (e + 1) * HEAD_DIM), s, vt)

    sh = (HEAD_DIM, HEAD_DIM)

    def by_column(a):
        drain(pbuf.at[a], prs.at[a])

        @pl.loop(0, NG, unroll=NG)
        def _(gg):
            y = nn(perm[...], pbuf[a, pl.ds(2 * gg, 2)].reshape(COLS, HEAD_DIM))
            ybuf[a, :, gg] = y.astype(BF).reshape(BLOCK, 16, HEAD_DIM)

    def lse_lane(st, i):
        at = my_block(st) * BLOCK + i
        if STAGES[st][2] < HEAD_DIM:
            at = at + (iota(sh, 0) % 2) * STAGES[st][2]
        return iota(sh, 1) == at

    def column_weights(st):
        @pl.when(mine(st))
        def _():
            by_column(0)
            by_column(1)

            def row_of(i):
                return (i // 16) * 16 + (i % 8) * 2 + (i // 8) % 2

            causal = row_of(iota(sh, 1)) <= row_of(iota(sh, 0))
            lsrc[...] = jnp.zeros_like(lsrc)

            @pl.loop(0, BLOCK, unroll=UNROLL)
            def _(i):
                qc, kc = (ybuf[a, i].reshape(sh) for a in range(2))
                s = jnp.where(causal, nt(qc, kc) * TO_LOG2, -BIG)
                peak = jnp.max(s, axis=1, keepdims=True)
                wts[i] = jnp.exp2(s - peak).astype(BF)
                lsrc[...] = jnp.where(lse_lane(st, i), peak, lsrc[...])

    def column_values(st):
        first, count, _w = STAGES[st]

        @pl.when(mine(st))
        def _():
            by_column(2)
            one = jnp.ones(sh, BF)

            @pl.loop(0, BLOCK, unroll=UNROLL)
            def _(i):
                got = nn(wts[i], jnp.concatenate([ybuf[2, i].reshape(sh), one], axis=1))
                total = got[:, HEAD_DIM:]
                obuf[i] = (got[:, :HEAD_DIM] / total).astype(BF).reshape(NG, 16, HEAD_DIM)
                lsrc[...] = lsrc[...] + jnp.where(lse_lane(st, i), jnp.log2(total), 0.0)

            b = first + my_block(st)

            def give_back(gg):
                y = nn(perm[...], obuf[:, gg].reshape(COLS, HEAD_DIM))
                rbuf[2 * gg : 2 * gg + 2] = y.astype(BF).reshape(2, NZ, BLOCK, HEAD_DIM)

            def tile(d):
                return lsrc.at[pl.ds(pl.multiple_of(d * NZ, NZ), NZ)]

            def send_back(gg, cc):
                d = gg * 2 + cc
                device = {"rows": row_id(gg, z, cc)}
                remote(tile(d), lbuf.at[b], lss, lrs.at[st], device).start()
                remote(rbuf.at[d], cbuf.at[b], rss, rrs.at[st], device).start()

            for gg in range(NG):
                give_back(gg)

            @pl.loop(1, NG)
            def _(s):
                gg = lax.rem(g + s, NG)
                for cc in range(2):
                    send_back(gg, cc)

            send_back(g, 1 - c)
            local(rbuf.at[p], cbuf.at[b], rrs.at[st])
            local(tile(p), lbuf.at[b], lrs.at[st])

    def merge(st):
        first, count, width = STAGES[st]
        drain(lbuf.at[pl.ds(first, count)], lrs.at[st])
        drain(cbuf.at[pl.ds(first, count)], rrs.at[st])
        lse_all = jnp.sum(lbuf[first : first + count], axis=0)
        per = LANES // width
        for i in range(NZ // per):
            rows = range(per * i, per * i + per)
            lse = [lse_all[zz : zz + 1] for zz in rows]
            if per > 2:
                lse = [lse[0] + lse[1], lse[2] + lse[3]]
            lse = jnp.concatenate(lse, axis=1)
            m = mx[st, i, :1]
            peak = jnp.maximum(m, lse)
            near_w = jnp.exp2(m - peak)
            col_w = jnp.exp2(lse - peak)
            inv = 1.0 / (tot[st, i, :1] * near_w + col_w)
            col = [cbuf[first : first + count, zz].reshape(width, HEAD_DIM) for zz in rows]
            col_t = nt(eye1, jnp.concatenate(col, axis=0))
            out_t = acc[st, i] * (near_w * inv) + col_t * (col_w * inv)
            out = nt(eye, out_t.astype(BF)).astype(BF)
            abuf[per * i : per * i + per, static_cols(st)] = out.reshape(per, width, HEAD_DIM)
        cols = stage_cols(st)
        local(abuf.at[z, cols], home.at[cols, head_lanes(z)], ars.at[st])

        @each_z_mate
        def _(zz, device):
            remote(abuf.at[zz, cols], home.at[cols, head_lanes(z)], ass.at[st], ars.at[st], device).start()

    width = NZ * HEAD_DIM

    def project(st):
        cols = stage_cols(st)
        drain(home.at[cols], ars.at[st])
        ours = pl.ds(pl.multiple_of(t * width, width), width)
        part = width // 2
        for e in range(2):
            theirs = pl.ds(pl.multiple_of((1 - t) * width + e * part, part), part)
            lanes = pl.ds(e * part, part)
            xsend[cols, lanes] = nn(home[cols], wbuf[:, theirs]).astype(BF)
            src, dst = xsend.at[cols, lanes], xrecv.at[cols, lanes]
            remote(src, dst, xss.at[st], xrs.at[st], {"heads": 1 - t}).start()
        own[cols] = nn(home[cols], wbuf[:, ours])

    def finish(st):
        cols = stage_cols(st)
        drain(xrecv.at[cols], xrs.at[st])
        res[cols] = (own[cols] + xrecv[cols].astype(F32)).astype(BF)
        local(res.at[cols], o_ref.at[cols], loc.at[3 + st])

    Q, K, V = range(3)
    share_summary()
    forward(Q, 0)
    share_summary_cores()
    forward(K, 0)
    drain(sg.at[1 - c], grs.at[1])
    summary(0, 0, 4)
    summary(0, 1, 4)
    summary(0, 2, 4)
    forward(V, 0)
    summary(0, 3, 4)
    near(0)
    forward(Q, 1)
    column_weights(0)
    forward(K, 1)
    summary(1, 0, 2)
    column_values(0)
    forward(V, 1)
    summary(1, 1, 2)
    forward(Q, 2)
    forward(K, 2)
    column_weights(1)
    near(1)
    forward(V, 2)
    column_values(1)
    summary(2, 0, 2)
    merge(0)
    summary(2, 1, 2)
    column_weights(2)
    column_values(2)
    near(2)
    merge(1)
    w_load.wait()
    project(0)
    merge(2)
    project(1)
    project(2)
    finish(0)
    finish(1)
    finish(2)

    drain(sz.at[:, pl.ds(0, NZ - 1)], zss.at[chunks])
    drain(sg.at[0, :, pl.ds(0, NG - 1)], gss.at[0])
    drain(sg.at[c], gss.at[1])
    for ch in range(len(NEXT), chunks):
        chunk_left(ch)
    for st, (first, count, _w) in enumerate(STAGES):
        for a in range(3):

            @pl.when(mine(st))
            def _():
                drain(pbuf.at[a, pl.ds(0, count - 1)], pss.at[a, st])

            @pl.when(jnp.logical_not(mine(st)))
            def _():
                drain(pbuf.at[a, pl.ds(0, count)], pss.at[a, st])

        cols = stage_cols(st)
        drain(abuf.at[pl.ds(0, NZ - 1), cols], ass.at[st])
        drain(xsend.at[cols], xss.at[st])
        pltpu.make_async_copy(res.at[cols], o_ref.at[cols], loc.at[3 + st]).wait()
    drain(rbuf.at[pl.ds(0, 2 * NG - 1)], rss)
    drain(lsrc.at[pl.ds(0, (2 * NG - 1) * NZ)], lss)


def on_device(queries, keys, values, summary_cols, w_out):
    width = queries.shape[1]
    any_space = pl.BlockSpec(memory_space=pl.ANY)
    dma = pltpu.SemaphoreType.DMA
    vmem = pltpu.VMEM
    e = HEAD_DIM
    n = len(STAGES)
    return pl.pallas_call(
        body,
        out_shape=jax.ShapeDtypeStruct(queries.shape, BF),
        in_specs=[pl.BlockSpec(memory_space=pltpu.SMEM)] + [any_space] * 4,
        out_specs=any_space,
        scratch_shapes=[
            vmem((3, NZ, COLS, e), BF),
            vmem((3, 2 * NG, NZ, BLOCK, e), BF),
            vmem((3, BLOCK, NG, 16, e), BF),
            vmem((BLOCK, e, e), BF),
            vmem((BLOCK, NG, 16, e), BF),
            vmem((2 * NG, NZ, BLOCK, e), BF),
            vmem((2 * NG, NZ, BLOCK, e), BF),
            vmem((NZ, COLS, e), BF),
            vmem((COLS, width), BF),
            vmem(w_out.shape, BF),
            vmem((2, COLS, width), BF),
            vmem((2, SUMS, width), BF),
            vmem((2, NZ, SUMS, e), BF),
            vmem((2, 2, NG, NZ, SUMS, e), BF),
            vmem((NZ, COLS, e), BF),
            vmem((3, COLS, e), BF),
            vmem((COLS, COLS), BF),
            vmem((e, e), F32),
            vmem((2 * NG, NZ, e), F32),
            vmem((n, NZ // 2, e, LANES), F32),
            vmem((n, NZ // 2, 8, LANES), F32),
            vmem((n, NZ // 2, 8, LANES), F32),
            vmem((COLS, width), F32),
            vmem((COLS, width), BF),
            vmem((COLS, width), BF),
            vmem((COLS, width), BF),
            dma((3 * n + 1,)), dma((3 * n + 1,)),
            dma((2,)), dma((2,)),
            dma((3, n)), dma((3,)),
            dma, dma((n,)),
            dma, dma((n,)),
            dma((n,)), dma((n,)),
            dma((n,)), dma((n,)),
            dma((3 + n,)),
        ],
        name="strided_attention",
        compiler_params=pltpu.CompilerParams(
            collective_id=0, has_side_effects=True, vmem_limit_bytes=53 * 1024 * 1024
        ),
    )(summary_cols, queries, keys, values, w_out)


def solution(mesh):
    return jax.shard_map(
        on_device,
        mesh=mesh,
        in_specs=(P("rows", "heads"), P("rows", "heads"), P("rows", "heads"), P(), P("heads", None)),
        out_specs=P("rows", "heads"),
        check_vma=False,
    )
```
